128 devices in a mesh: section: 2 (over z_lo), chan: 8 (over x, z_hi), batch: 8 (over y, core).
Axes of the slice: x: 4, y: 4, z: 4 (z_hi: 2, z_lo: 2; z = z_hi * 2 + z_lo), core: 2. Of those that a mesh axis runs over, the one named last changes fastest.
Arguments:
- images: bfloat16 [2, 8, 8, 256, 1024], P('section', 'batch', 'chan'), may hold values from -12 to 12
- w_early: bfloat16 [1024, 2048], replicated, may hold values from -0.1875 to 0.1875
- gain_early: float32 [2048], replicated, may hold values from 0.5 to 1.5
- bias_early: float32 [2048], replicated, may hold values from -0.5 to 0.5
- w_late: bfloat16 [2048, 8192], P(None, 'chan'), may hold values from -0.125 to 0.125
- gain_late: float32 [8192], P('chan'), may hold values from 0.5 to 1.5
- bias_late: float32 [8192], P('chan'), may hold values from -0.5 to 0.5
- cotangent: bfloat16 [2, 64, 256, 8192], P('section', 'batch', None, 'chan'), may hold values from -6 to 6
Outputs:
- late_out: bfloat16 [2, 64, 256, 8192], P('section', 'batch', None, 'chan')
- grad_late: float32 [2048, 8192], P(None, 'chan')
- grad_early: float32 [1024, 2048], P(('section', 'chan', 'batch'))
The draws below stay inside these ranges and needn't reach their ends.
All inputs are finite; a program needn't handle non-finite values.
Results may differ from the reference program's by a relative error of at most 0.024.
Values may be sent and summed in bfloat16 or wider, within the bound.
No kernel may reach another device: no remote copies, remote signals or barrier semaphores. Data moves between devices by JAX's collectives and lax.ppermute only.
A program may use at most 192 MiB of HBM per device.

```python
import jax
import jax.numpy as jnp
from jax import lax

E = 1024
A = 2048
L = 8192
PIX = 256
IMG_DEV = 1
IMAGES = 64
MICRO = 2
N_CHAN = 8
N_BATCH = 8


def draw_images(key, part):
    key = jax.random.fold_in(key, 11)
    key_base, key_scale, key_shared, key_own, key_rate = jax.random.split(key, 5)
    shape = (MICRO, N_BATCH, N_CHAN * IMG_DEV, PIX, E)
    batch_pos = jnp.arange(N_BATCH, dtype=jnp.float32).reshape(1, N_BATCH, 1, 1, 1)
    chan_pos = (jnp.arange(N_CHAN * IMG_DEV, dtype=jnp.float32) // IMG_DEV).reshape(1, 1, N_CHAN * IMG_DEV, 1, 1)
    order = (chan_pos * N_BATCH + batch_pos) / (N_CHAN * N_BATCH - 1)
    image_scale = jnp.exp(jax.random.uniform(key_scale, (MICRO, N_BATCH, N_CHAN * IMG_DEV, 1, 1), jnp.float32, -0.8, 0.8))
    shared = jax.random.uniform(key_shared, (1, 1, 1, 1, E), jnp.float32, -1.0, 1.0)
    own = 0.3 * jax.random.normal(key_own, (MICRO, N_BATCH, N_CHAN * IMG_DEV, 1, E), jnp.float32)
    base = jnp.clip(jax.random.normal(key_base, shape, jnp.float32), -4.0, 4.0)
    rate = jax.random.uniform(key_rate, (), jnp.float32, 1.0986123, 1.6094379)
    values = 0.5 * (base + shared + own) * jnp.exp(order * rate) * image_scale
    return jnp.clip(values, -12.0, 12.0).astype(jnp.bfloat16)


def block_scale(stream_key, dims, cuts, least, top_value):
    loudness, own = 1.0, jax.random.fold_in(stream_key, 6)
    for position, shards_of in cuts:
        heights = jnp.exp(jax.random.uniform(jax.random.fold_in(own, position), (shards_of,), jnp.float32, least / len(cuts), top_value / len(cuts)))
        loudness = loudness * jnp.repeat(heights, dims[position] // shards_of).reshape([-1 if axis == position else 1 for axis in range(len(dims))])
    return loudness


def centred(key, extent, width, bound, pieces=(), kind=jnp.bfloat16):
    level = block_scale(key, extent, pieces, -0.22, 0.18) if pieces else 1.0
    result = jax.random.normal(key, extent, jnp.float32) * width * level
    return jnp.minimum(jnp.maximum(result, -bound), bound).astype(kind)


def setup_inputs(seed: int = 0) -> dict:
    arg_keys = jax.random.split(jax.random.key(seed), 9)
    images = draw_images(jax.random.fold_in(arg_keys[8], 71), 0)
    w_early = centred(arg_keys[1], (E, A), E ** -0.5, 0.1875)
    gain_early = jnp.clip(jax.random.uniform(arg_keys[2], (A,), jnp.float32, 0.5, 1.5), 0.5, 1.5)
    bias_early = jnp.clip(jax.random.uniform(arg_keys[3], (A,), jnp.float32, -0.5, 0.5), -0.5, 0.5)
    w_late = centred(arg_keys[4], (A, L), A ** -0.5, 0.125, ((1, 8),))
    gain_late = jnp.clip(0.5 + 1.0 * jax.random.uniform(arg_keys[5], (L,), jnp.float32) ** block_scale(arg_keys[5], (L,), ((0, 8),), -0.2, 0.2), 0.5, 1.5)
    bias_late = jnp.clip(jax.random.uniform(arg_keys[6], (L,), jnp.float32, -0.5, 0.5) * block_scale(arg_keys[6], (L,), ((0, 8),), -0.4, 0.0), -0.5, 0.5)
    cotangent = centred(arg_keys[7], (MICRO, IMAGES, PIX, L), 1.0, 6.0, ((0, 2), (1, 8), (3, 8)))
    return dict(images=images, w_early=w_early, gain_early=gain_early, bias_early=bias_early, w_late=w_late, gain_late=gain_late, bias_late=bias_late, cotangent=cotangent)


def smooth_gate(values):
    return values * jax.nn.sigmoid(values)

def smooth_slope(values):
    sig = jax.nn.sigmoid(values)
    return sig * (1.0 + values * (1.0 - sig))

def norm_forward(values, gain, bias):
    count = values.shape[0]
    mean = lax.optimization_barrier(jnp.sum(values, 0)) / count
    rstd = lax.rsqrt(lax.optimization_barrier(jnp.sum(values * values, 0)) / count - mean * mean + 1e-05)
    normed = (values - mean) * rstd
    return (normed, rstd, normed * gain + bias)

def norm_backward(grad, normed, rstd, gain):
    count = grad.shape[0]
    first = lax.optimization_barrier(jnp.sum(grad, 0)) / count
    second = lax.optimization_barrier(jnp.sum(grad * normed, 0)) / count
    return gain * rstd * (grad - first - normed * second)

def reference(images, w_early, gain_early, bias_early, w_late, gain_late, bias_late, cotangent):
    micro = images.shape[0]
    width_in = images.shape[4]
    width_mid = w_early.shape[1]
    width_out = w_late.shape[1]
    group = width_out // N_CHAN
    image_total = images.shape[1] * images.shape[2]
    outputs = []
    grad_late = jnp.zeros((width_mid, width_out), jnp.float32)
    grad_early = jnp.zeros((width_in, width_mid), jnp.float32)
    for index in range(micro):
        flat_in = images[index].reshape(-1, width_in)
        raw = jnp.dot(flat_in, w_early, preferred_element_type=jnp.float32).astype(jnp.bfloat16)
        normed_e, rstd_e, pre_e = norm_forward(raw.astype(jnp.float32), gain_early, bias_early)
        act = smooth_gate(pre_e).astype(jnp.bfloat16)
        hidden = jnp.dot(act, w_late, preferred_element_type=jnp.float32)
        normed_l, rstd_l, pre_l = norm_forward(hidden, gain_late, bias_late)
        outputs.append(smooth_gate(pre_l).astype(jnp.bfloat16).reshape(image_total, images.shape[3], width_out))
        grad_y = cotangent[index].reshape(-1, width_out).astype(jnp.float32) * smooth_slope(pre_l)
        grad_h = norm_backward(grad_y, normed_l, rstd_l, gain_late).astype(jnp.bfloat16)
        grad_late = grad_late + jnp.dot(act.T, grad_h, preferred_element_type=jnp.float32)
        grad_act = jnp.zeros((flat_in.shape[0], width_mid), jnp.float32)
        for block in range(N_CHAN):
            part = jnp.dot(grad_h[:, block * group:(block + 1) * group], w_late[:, block * group:(block + 1) * group].T, preferred_element_type=jnp.float32)
            grad_act = grad_act + part.astype(jnp.bfloat16).astype(jnp.float32)
        grad_pre = grad_act * smooth_slope(pre_e)
        grad_raw = norm_backward(grad_pre, normed_e, rstd_e, gain_early).astype(jnp.bfloat16)
        grad_early = grad_early + jnp.dot(flat_in.T, grad_raw, preferred_element_type=jnp.float32)
    return (jnp.stack(outputs), grad_late, grad_early)
```

```python
import jax
import jax.numpy as jnp
from jax import lax
from jax.sharding import PartitionSpec as P

BF = jnp.bfloat16
F32 = jnp.float32


def shift(value, axis, step):
    return lax.ppermute(
        value, axis, [(i, ((i // 2 - step) % 4) * 2 + i % 2) for i in range(8)]
    )


def swap(value, axis):
    size = 2 if axis == "section" else 8
    return lax.ppermute(value, axis, [(i, i ^ 1) for i in range(size)])


def sum_pair(value, axis):
    return value + swap(value, axis)


def sum_ring(value, axis):
    one, two, three = (shift(value, axis, step) for step in (1, 2, 3))
    return (value + two) + (one + three)


def sum_batch(value):
    return sum_ring(sum_pair(value, "batch"), "batch")


def sum_all(value):
    return sum_pair(sum_ring(sum_batch(value), "chan"), "chan")


def block_of(value, index, rows):
    return lax.dynamic_slice_in_dim(value, index * rows, rows, 0)


def scatter_pair(value, axis, mine):
    rows = value.shape[0] // 2
    other = swap(block_of(value, 1 - mine, rows), axis)
    return block_of(value, mine, rows).astype(F32) + other.astype(F32)


def scatter_ring(value, axis, mine):
    rows = value.shape[0] // 4
    parts = [
        shift(block_of(value, (mine - step) % 4, rows), axis, step).astype(F32)
        for step in (1, 2, 3)
    ]
    return (block_of(value, mine, rows).astype(F32) + parts[1]) + (parts[0] + parts[2])


def gather_ring(value, axis, mine):
    rows = value.shape[0]
    full = jnp.zeros((4 * rows,) + value.shape[1:], value.dtype)
    full = lax.dynamic_update_slice_in_dim(full, value, mine * rows, 0)
    for step in (1, 2, 3):
        full = lax.dynamic_update_slice_in_dim(
            full, shift(value, axis, step), (mine + step) % 4 * rows, 0
        )
    return full


def gather_pair(value, axis, mine):
    other = swap(value, axis)
    first = jnp.where(mine == 0, value, other)
    second = jnp.where(mine == 0, other, value)
    return jnp.concatenate([first, second], 0)


def fwd_block(rows, w_early, w_late, scale, offset):
    raw = jnp.dot(rows, w_early, preferred_element_type=F32)
    pre = raw * scale + offset
    sig = jax.nn.sigmoid(pre)
    act = pre * sig
    slope = (sig + act * (1.0 - sig)).astype(BF)
    act = act.astype(BF)
    late = jnp.dot(act, w_late, preferred_element_type=F32)
    return raw.astype(BF), act, slope, late, jnp.stack([jnp.sum(late, 0), jnp.sum(late * late, 0)])


def body(images, w_early, gain_early, bias_early, w_late, gain_late, bias_late, cotangent):
    width_in, width_mid = w_early.shape
    width_out = w_late.shape[1]
    pixels = images.shape[3]
    own = images.reshape(pixels, width_in)
    chan = lax.axis_index("chan")
    batch = lax.axis_index("batch")
    x_pos, z_pos = chan // 2, chan % 2
    y_pos, core = batch // 2, batch % 2
    count = float(pixels * 64)

    raw_own = jnp.dot(own, w_early, preferred_element_type=F32).astype(BF).astype(F32)
    sums_e = sum_all(jnp.stack([jnp.sum(raw_own, 0), jnp.sum(raw_own * raw_own, 0)]))
    mean_e = sums_e[0] / count
    rstd_e = lax.rsqrt(sums_e[1] / count - mean_e * mean_e + 1e-05)
    scale_e = rstd_e * gain_early
    offset_e = bias_early - mean_e * scale_e

    half = pixels // 2
    right = shift(own, "chan", 1)
    left = shift(own, "chan", 3)
    deep = swap(own, "chan")
    far = jnp.concatenate([shift(right[:half], "chan", 1), shift(left[half:], "chan", 3)], 0)
    deep_right = shift(deep, "chan", 1)
    deep_left = shift(deep, "chan", 3)
    deep_far = swap(far, "chan")
    order = [
        ((x_pos + dx) % 4) * 2 + (z_pos ^ dz)
        for dx, dz in ((0, 0), (1, 0), (3, 0), (0, 1), (2, 0), (1, 1), (3, 1), (2, 1))
    ]
    groups = [
        jnp.concatenate([own, right, left, deep], 0),
        jnp.concatenate([far, deep_right, deep_left], 0),
        deep_far,
    ]
    done = [fwd_block(rows, w_early, w_late, scale_e, offset_e) for rows in groups]
    rows_all = jnp.concatenate(groups, 0)
    raw, act, slope, late = (jnp.concatenate([d[k] for d in done], 0) for k in range(4))
    sums_l = sum_batch(done[0][4] + done[1][4] + done[2][4])
    mean_l = sums_l[0] / count
    rstd_l = lax.rsqrt(sums_l[1] / count - mean_l * mean_l + 1e-05)

    cot = cotangent.reshape(8, pixels, width_out)
    cot = jnp.concatenate([lax.dynamic_index_in_dim(cot, j, 0, False) for j in order], 0)
    normed_l = (late - mean_l) * rstd_l
    pre_l = normed_l * gain_late + bias_late
    sig_l = jax.nn.sigmoid(pre_l)
    out_l = pre_l * sig_l
    grad_y = cot.astype(F32) * (sig_l + out_l * (1.0 - sig_l))
    back = sum_batch(jnp.stack([jnp.sum(grad_y, 0), jnp.sum(grad_y * normed_l, 0)])) / count
    grad_h = (gain_late * rstd_l * (grad_y - back[0] - normed_l * back[1])).astype(BF)
    out_rel = out_l.astype(BF).reshape(8, pixels, width_out)
    late_out = jnp.zeros_like(out_rel)
    for k, j in enumerate(order):
        late_out = lax.dynamic_update_slice_in_dim(late_out, out_rel[k : k + 1], j, 0)
    late_out = late_out.reshape(cotangent.shape)

    pieces = []
    for cols in jnp.split(grad_h, 2, axis=1):
        part = lax.dot_general(
            act, cols, (((0,), (0,)), ((), ())), preferred_element_type=F32
        ).astype(BF)
        part = scatter_pair(part, "batch", core).astype(BF)
        part = scatter_ring(part, "batch", y_pos).astype(BF)
        part = sum_pair(part.astype(F32).astype(BF), "section")
        part = gather_ring(part, "batch", y_pos)
        pieces.append(gather_pair(part, "batch", core))
    grad_late = jnp.concatenate(pieces, 1).astype(F32)

    rows_cut = rows_all.reshape(-1, 2, 4, 2, 4, 2, 8)
    rows_cut = jnp.transpose(rows_cut, (0, 5, 2, 3, 4, 1, 6)).reshape(-1, width_in)
    parts, sums_g = [], []
    step = width_mid // 4
    for k in range(4):
        cut = slice(k * step, (k + 1) * step)
        grad_act = lax.dot_general(
            grad_h, w_late[cut], (((1,), (1,)), ((), ())), preferred_element_type=F32
        )
        grad_pre = grad_act * slope[:, cut].astype(F32)
        sums_g.append(
            jnp.stack([jnp.sum(grad_pre, 0), jnp.sum(grad_pre * raw[:, cut].astype(F32), 0)])
        )
        term = lax.dot_general(
            rows_cut,
            grad_pre.astype(BF),
            (((0,), (0,)), ((), ())),
            preferred_element_type=F32,
        ).astype(BF)
        term = scatter_pair(term, "batch", core).astype(BF)
        parts.append(scatter_ring(term, "chan", x_pos).astype(BF))
    sums_g = sum_all(jnp.concatenate(sums_g, 1)) / count
    back_one = sums_g[0]
    back_two = rstd_e * (sums_g[1] - mean_e * sums_g[0])
    grad = scatter_pair(jnp.concatenate(parts, 1), "chan", z_pos)

    here = rows_cut.reshape(-1, 2, 8, 64)
    here = lax.dynamic_index_in_dim(here, chan, 2, False).reshape(-1, 128)
    cross = lax.dot_general(here, raw, (((0,), (0,)), ((), ())), preferred_element_type=F32)
    colsum = jnp.sum(here.astype(F32), 0)
    cross = jnp.concatenate([cross, jnp.broadcast_to(colsum[:, None], (128, 128))], 1)
    cross = scatter_pair(cross, "batch", core)
    colsum = cross[:, width_mid:][:, :1]
    cross = rstd_e * (cross[:, :width_mid] - colsum * mean_e)
    grad = scale_e * (grad - colsum * back_one - cross * back_two)
    grad = scatter_ring(grad, "batch", y_pos)
    section = lax.axis_index("section")
    grad_early = scatter_pair(grad, "section", section)
    return (late_out, grad_late, grad_early)


def solution(mesh):
    return jax.shard_map(
        body,
        mesh=mesh,
        in_specs=(
            P("section", "batch", "chan", None, None),
            P(),
            P(),
            P(),
            P(None, "chan"),
            P("chan"),
            P("chan"),
            P("section", "batch", None, "chan"),
        ),
        out_specs=(
            P("section", "batch", None, "chan"),
            P(None, "chan"),
            P(("section", "chan", "batch"), None),
        ),
        check_vma=False,
    )
```

```python
import functools

import jax
import jax.numpy as jnp
from jax import lax
from jax.experimental import pallas as pl
from jax.experimental.pallas import tpu as pltpu
from jax.sharding import PartitionSpec as P

BF = jnp.bfloat16
F32 = jnp.float32
MIB = 1 << 20


def shift(value, axis, step):
    return lax.ppermute(
        value, axis, [(i, ((i // 2 - step) % 4) * 2 + i % 2) for i in range(8)]
    )


def swap(value, axis):
    size = 2 if axis == "section" else 8
    return lax.ppermute(value, axis, [(i, i ^ 1) for i in range(size)])


def sum_pair(value, axis):
    return value + swap(value, axis)


def sum_ring(value, axis):
    one, two, three = (shift(value, axis, step) for step in (1, 2, 3))
    return (value + two) + (one + three)


def sum_batch(value):
    return sum_ring(sum_pair(value, "batch"), "batch")


def sum_all(value):
    return sum_pair(sum_ring(sum_batch(value), "chan"), "chan")


def scatter_pair(value, axis):
    rows = value.shape[0] // 2
    return value[:rows].astype(F32) + swap(value[rows:], axis).astype(F32)


def scatter_ring(value, axis):
    rows = value.shape[0] // 4
    one, two, three = (
        shift(value[k * rows : (k + 1) * rows], axis, -k).astype(F32) for k in (1, 2, 3)
    )
    return (value[:rows].astype(F32) + two) + (one + three)


def gather_ring(value, axis):
    return jnp.concatenate([value] + [shift(value, axis, k) for k in (1, 2, 3)], 0)


def sigmoid(value):
    return 0.5 * jnp.tanh(0.5 * value) + 0.5


def params(mib):
    return pltpu.CompilerParams(vmem_limit_bytes=mib * MIB)


def fwd_kernel(place, raw, scale, offset, w_late, *refs):
    act_t, slope, late, sums = refs[-4:]
    total = None
    for c in range(0, raw.shape[1], 256):
        pre = raw[:, c : c + 256].astype(F32) * scale[:, c : c + 256] + offset[:, c : c + 256]
        sig = sigmoid(pre)
        act = pre * sig
        slope[:, c : c + 256] = (sig + act * (1.0 - sig)).astype(BF)
        act = act.astype(BF)
        turned = act.T
        for s in (0, 128):
            act_t[pl.ds(pl.multiple_of(place[(c + s) // 128] * 128, 128), 128), :] = turned[
                s : s + 128
            ]
        part = jnp.dot(act, w_late[c : c + 256, :], preferred_element_type=F32)
        total = part if total is None else total + part
    late[...] = total

    @pl.when(pl.program_id(0) == 0)
    def _():
        sums[...] = jnp.zeros_like(sums)

    sums[0:1] += jnp.sum(total, 0, keepdims=True)
    sums[1:2] += jnp.sum(total * total, 0, keepdims=True)


def fwd_blocks(place, raw, scale, offset, w_late, first, full, earlier=None):
    count = raw.shape[0] // 256
    mid, out = w_late.shape
    rows = full * 256
    shapes = (
        jax.ShapeDtypeStruct((mid, rows), BF),
        jax.ShapeDtypeStruct((rows, mid), BF),
        jax.ShapeDtypeStruct((rows, out), F32),
        jax.ShapeDtypeStruct((8, out), F32),
    )
    extra = () if earlier is None else tuple(earlier)
    return pl.pallas_call(
        fwd_kernel,
        out_shape=shapes,
        grid_spec=pltpu.PrefetchScalarGridSpec(
            num_scalar_prefetch=1,
            grid=(count,),
            in_specs=[
                pl.BlockSpec((256, mid), lambda i, p: (i, 0)),
                pl.BlockSpec((1, mid), lambda i, p: (0, 0)),
                pl.BlockSpec((1, mid), lambda i, p: (0, 0)),
                pl.BlockSpec(memory_space=pltpu.VMEM),
            ]
            + [pl.BlockSpec(memory_space=pl.ANY)] * len(extra),
            out_specs=[
                pl.BlockSpec((mid, 256), lambda i, p: (0, i + first)),
                pl.BlockSpec((256, mid), lambda i, p: (i + first, 0)),
                pl.BlockSpec((256, out), lambda i, p: (i + first, 0)),
                pl.BlockSpec((8, out), lambda i, p: (0, 0)),
            ],
        ),
        input_output_aliases={5 + k: k for k in range(len(extra))},
        cost_estimate=pl.CostEstimate(
            flops=2 * count * 256 * mid * out,
            bytes_accessed=count * 256 * (mid * 6 + out * 4) + 2 * mid * out,
            transcendentals=count * 256 * mid,
        ),
        compiler_params=params(32),
    )(place, raw, scale, offset, w_late, *extra)


def late_kernel(order, late, cot, scale, offset, out, grad, sums):
    @pl.when(pl.program_id(0) == 0)
    def _():
        sums[...] = jnp.zeros_like(sums)

    def step(k, carry):
        one, two = carry
        at = pl.ds(pl.multiple_of(k * 16, 16), 16)
        value = late[at, :]
        pre = value * scale[...] + offset[...]
        sig = sigmoid(pre)
        gate = pre * sig
        out[0, at, :] = gate.astype(BF)
        grad_y = cot[0, at, :].astype(F32) * (sig + gate * (1.0 - sig))
        grad[at, :] = grad_y.astype(BF)
        both = grad_y * value
        return one + grad_y[:8] + grad_y[8:], two + both[:8] + both[8:]

    zero = jnp.zeros((8, late.shape[1]), F32)
    one, two = lax.fori_loop(0, late.shape[0] // 16, step, (zero, zero), unroll=2)
    sums[0:1] += jnp.sum(one, 0, keepdims=True)
    sums[1:2] += jnp.sum(two, 0, keepdims=True)


def late_pass(order, late, cot, scale, offset):
    rows, width = late.shape
    count = rows // 256
    return pl.pallas_call(
        late_kernel,
        out_shape=(
            jax.ShapeDtypeStruct(cot.shape, BF),
            jax.ShapeDtypeStruct((rows, width), BF),
            jax.ShapeDtypeStruct((8, width), F32),
        ),
        grid_spec=pltpu.PrefetchScalarGridSpec(
            num_scalar_prefetch=1,
            grid=(count,),
            in_specs=[
                pl.BlockSpec((256, width), lambda i, o: (i, 0)),
                pl.BlockSpec((1, 256, width), lambda i, o: (o[i], 0, 0)),
                pl.BlockSpec((1, width), lambda i, o: (0, 0)),
                pl.BlockSpec((1, width), lambda i, o: (0, 0)),
            ],
            out_specs=[
                pl.BlockSpec((1, 256, width), lambda i, o: (o[i], 0, 0)),
                pl.BlockSpec((256, width), lambda i, o: (i, 0)),
                pl.BlockSpec((8, width), lambda i, o: (0, 0)),
            ],
        ),
        cost_estimate=pl.CostEstimate(
            flops=16 * rows * width, bytes_accessed=rows * width * 10, transcendentals=rows * width
        ),
        compiler_params=params(32),
    )(order, late, cot, scale, offset)


def early_kernel(grad_h, turned, w_late, slope, raw, term, sums, grad_pre):
    one = two = 0.0
    for r in range(0, grad_h.shape[0], 512):
        grad = lax.dot_general(
            grad_h[r : r + 512, :],
            w_late[...],
            (((1,), (1,)), ((), ())),
            preferred_element_type=F32,
        )
        grad = grad * slope[r : r + 512, :].astype(F32)
        one += jnp.sum(grad, 0, keepdims=True)
        two += jnp.sum(grad * raw[r : r + 512, :].astype(F32), 0, keepdims=True)
        grad_pre[r : r + 512, :] = grad.astype(BF)
    sums[0:1] = one
    sums[1:2] = two
    for m in range(0, turned.shape[0], 512):
        term[m : m + 512, :] = jnp.dot(
            turned[m : m + 512, :], grad_pre[...], preferred_element_type=F32
        ).astype(BF)


def early_grad(grad_h, turned, w_late, slope, raw, first, width):
    rows, out = grad_h.shape
    tile = 256
    base = first // tile
    return pl.pallas_call(
        early_kernel,
        grid=(width // tile,),
        out_shape=(
            jax.ShapeDtypeStruct((turned.shape[0], width), BF),
            jax.ShapeDtypeStruct((8, width), F32),
        ),
        in_specs=[
            pl.BlockSpec(memory_space=pltpu.VMEM),
            pl.BlockSpec(memory_space=pltpu.VMEM),
            pl.BlockSpec((tile, out), lambda j: (j + base, 0)),
            pl.BlockSpec((rows, tile), lambda j: (0, j + base)),
            pl.BlockSpec((rows, tile), lambda j: (0, j + base)),
        ],
        out_specs=[
            pl.BlockSpec((turned.shape[0], tile), lambda j: (0, j)),
            pl.BlockSpec((8, tile), lambda j: (0, j)),
        ],
        scratch_shapes=[pltpu.VMEM((rows, tile), BF)],
        cost_estimate=pl.CostEstimate(
            flops=2 * rows * width * (out + turned.shape[0]),
            bytes_accessed=2 * (rows * out + rows * turned.shape[0] + 4 * rows * width),
            transcendentals=0,
        ),
        compiler_params=params(36),
    )(grad_h, turned, w_late, slope, raw)


def place_kernel(spots, mine, other, *refs):
    out = refs[-1]

    @pl.when(pl.program_id(0) == 0)
    def _():
        out[...] = mine[...].astype(F32)

    @pl.when(pl.program_id(0) == 1)
    def _():
        out[...] = other[...].astype(F32)


def place_rows(spots, mine, other, rows, earlier=None):
    width = mine.shape[1]
    extra = () if earlier is None else (earlier,)
    return pl.pallas_call(
        place_kernel,
        out_shape=jax.ShapeDtypeStruct((rows, width), F32),
        grid_spec=pltpu.PrefetchScalarGridSpec(
            num_scalar_prefetch=1,
            grid=(2, 4),
            in_specs=[
                pl.BlockSpec((128, width), lambda h, i, s: (jnp.where(h == 0, i, 3), 0)),
                pl.BlockSpec((128, width), lambda h, i, s: (jnp.where(h == 0, 0, i), 0)),
            ]
            + [pl.BlockSpec(memory_space=pl.ANY)] * len(extra),
            out_specs=pl.BlockSpec((128, width), lambda h, i, s: (s[h * 4 + i], 0)),
        ),
        input_output_aliases={3: 0} if extra else {},
        cost_estimate=pl.CostEstimate(
            flops=0, bytes_accessed=1024 * width * 6, transcendentals=0
        ),
        compiler_params=params(16),
    )(spots, mine, other, *extra)


def body(images, w_early, gain_early, bias_early, w_late, gain_late, bias_late, cotangent):
    width_in, width_mid = w_early.shape
    width_out = w_late.shape[1]
    pixels = images.shape[3]
    own = images.reshape(pixels, width_in)
    chan = lax.axis_index("chan")
    batch = lax.axis_index("batch")
    section = lax.axis_index("section")
    x_pos, z_pos = chan // 2, chan % 2
    y_pos, core = batch // 2, batch % 2
    count = float(pixels * 64)

    half = pixels // 2
    deep = swap(own, "chan")
    right = shift(own, "chan", 1)
    left = shift(own, "chan", 3)

    raw_own = jnp.dot(own, w_early, preferred_element_type=F32)
    sums_e = sum_all(jnp.stack([jnp.sum(raw_own, 0), jnp.sum(raw_own * raw_own, 0)]))
    mean_e = sums_e[0] / count
    rstd_e = lax.rsqrt(sums_e[1] / count - mean_e * mean_e + 1e-05)
    scale_e = rstd_e * gain_early
    offset_e = bias_early - mean_e * scale_e

    far = jnp.concatenate([shift(right[:half], "chan", 1), shift(left[half:], "chan", 3)], 0)
    deep_right = shift(deep, "chan", 1)
    deep_left = shift(deep, "chan", 3)
    deep_far = swap(far, "chan")
    order = jnp.stack(
        [
            ((x_pos + dx) % 4) * 2 + (z_pos ^ dz)
            for dx, dz in ((0, 0), (1, 0), (3, 0), (0, 1), (2, 0), (1, 1), (3, 1), (2, 1))
        ]
    ).astype(jnp.int32)

    tiles = jnp.arange(16, dtype=jnp.int32)
    t_core, t_y, t_half = tiles // 8, (tiles // 2) % 4, tiles % 2
    place = t_half * 8 + (t_core ^ core) * 4 + (t_y - y_pos) % 4
    spots = jnp.stack(
        [
            jnp.stack([((core ^ dc) * 4 + (y_pos + dy) % 4) * 2 + q for dc in (0, 1) for dy in range(4)])
            for q in (0, 1)
        ]
    ).astype(jnp.int32)

    groups = [
        jnp.concatenate([own, right, left, deep], 0),
        jnp.concatenate([far, deep_right, deep_left], 0),
        deep_far,
    ]
    raws, state, sums_l, first = [], None, 0.0, 0
    for rows in groups:
        raw = jnp.dot(rows, w_early, preferred_element_type=F32).astype(BF)
        raws.append(raw)
        *state, sums = fwd_blocks(
            place, raw, scale_e[None], offset_e[None], w_late, first, 8, state
        )
        first += rows.shape[0] // 256
        sums_l += sums[:2]
    act_t, slope, late = state
    rows_all = jnp.concatenate(groups, 0)
    raw = jnp.concatenate(raws, 0)

    sums_l = sum_batch(sums_l) / count
    at = jnp.arange(width_in, dtype=jnp.int32)
    p_core, p_x, p_z = at // 512, (at // 128) % 4, (at // 64) % 2
    p_y, p_sec, p_row = (at // 16) % 4, (at // 8) % 2, at % 8
    source = (
        (p_sec ^ section) * 512
        + (((p_x + x_pos) % 4) * 2 + (p_z ^ z_pos)) * 64
        + (((p_y + y_pos) % 4) * 2 + (p_core ^ core)) * 8
        + p_row
    )
    pick = (source[:, None] == at[None, :]).astype(BF)
    turned = lax.dot_general(
        pick, rows_all, (((1,), (1,)), ((), ())), preferred_element_type=F32
    ).astype(BF)
    sums_l, turned = lax.optimization_barrier((sums_l, turned))

    mean_l = sums_l[0]
    rstd_l = lax.rsqrt(sums_l[1] - mean_l * mean_l + 1e-05)
    scale_l = rstd_l * gain_late
    offset_l = bias_late - mean_l * scale_l
    late_out, grad_y, back = late_pass(
        order, late, cotangent.reshape(8, pixels, width_out), scale_l[None], offset_l[None]
    )
    late_out = late_out.reshape(cotangent.shape)
    back = sum_batch(back[:2]) / count

    here = turned.reshape(2, 512, -1)[:, :64].reshape(128, -1)
    cross = jnp.dot(here, raw, preferred_element_type=F32)
    colsum = jnp.sum(here.astype(F32), 1)
    cross = jnp.concatenate([cross, jnp.broadcast_to(colsum[:, None], (128, 128))], 1)
    cross = scatter_pair(cross, "batch")
    back, cross = lax.optimization_barrier((back, cross))

    back_one = back[0]
    back_two = rstd_l * (back[1] - mean_l * back_one)
    by_late = -scale_l * rstd_l * back_two
    constant = -scale_l * back_one - mean_l * by_late
    grad_h = (grad_y.astype(F32) * scale_l + late * by_late + constant).astype(BF)

    cuts = [
        jnp.dot(cut, grad_h, preferred_element_type=F32).astype(BF)
        for cut in jnp.split(act_t, 2, axis=0)
    ]
    grad_h, *cuts = lax.optimization_barrier((grad_h, *cuts))
    grad_late = None
    for q, part in enumerate(cuts):
        part = scatter_pair(part, "batch").astype(BF)
        part = scatter_ring(part, "batch").astype(BF)
        part = sum_pair(part, "section")
        part = gather_ring(part, "batch")
        grad_late = place_rows(spots[q], part, swap(part, "batch"), width_mid, grad_late)

    parts, sums_g = [], []
    for k in range(2):
        step = width_mid // 2
        term, sums = early_grad(grad_h, turned, w_late, slope, raw, k * step, step)
        sums_g.append(sums[:2])
        term = scatter_pair(term, "batch").astype(BF)
        parts.append(scatter_ring(term, "chan").astype(BF))
    sums_g = sum_all(jnp.concatenate(sums_g, 1)) / count
    back_one = sums_g[0]
    back_two = rstd_e * (sums_g[1] - mean_e * sums_g[0])
    grad = scatter_pair(jnp.concatenate(parts, 1), "chan")
    colsum = cross[:, width_mid:][:, :1]
    cross = rstd_e * (cross[:, :width_mid] - colsum * mean_e)
    grad = scale_e * (grad - colsum * back_one - cross * back_two)
    grad = scatter_ring(grad, "batch")
    grad_early = scatter_pair(grad, "section")
    return (late_out, grad_late, grad_early)


def solution(mesh):
    return jax.shard_map(
        body,
        mesh=mesh,
        in_specs=(
            P("section", "batch", "chan", None, None),
            P(),
            P(),
            P(),
            P(None, "chan"),
            P("chan"),
            P("chan"),
            P("section", "batch", None, "chan"),
        ),
        out_specs=(
            P("section", "batch", None, "chan"),
            P(None, "chan"),
            P(("section", "chan", "batch"), None),
        ),
        check_vma=False,
    )
```

```python
import functools

import jax
import jax.numpy as jnp
from jax import lax
from jax.experimental import pallas as pl
from jax.experimental.pallas import tpu as pltpu
from jax.sharding import PartitionSpec as P

BF = jnp.bfloat16
F32 = jnp.float32
MIB = 1 << 20
LIMIT = 40


def shift(value, axis, step):
    return lax.ppermute(
        value, axis, [(i, ((i // 2 - step) % 4) * 2 + i % 2) for i in range(8)]
    )


def swap(value, axis):
    size = 2 if axis == "section" else 8
    return lax.ppermute(value, axis, [(i, i ^ 1) for i in range(size)])


def sum_pair(value, axis):
    return value + swap(value, axis)


def sum_ring(value, axis):
    one, two, three = (shift(value, axis, step) for step in (1, 2, 3))
    return (value + two) + (one + three)


def sum_batch(value):
    return sum_ring(sum_pair(value, "batch"), "batch")


def scatter_pair(value, axis):
    rows = value.shape[0] // 2
    return value[:rows].astype(F32) + swap(value[rows:], axis).astype(F32)


def scatter_ring(value, axis):
    rows = value.shape[0] // 4
    one, two, three = (
        shift(value[k * rows : (k + 1) * rows], axis, -k).astype(F32) for k in (1, 2, 3)
    )
    return (value[:rows].astype(F32) + two) + (one + three)


def tie(*values):
    return lax.optimization_barrier(values)


def sigmoid(value):
    return 0.5 * jnp.tanh(0.5 * value) + 0.5


def params(mib):
    return pltpu.CompilerParams(vmem_limit_bytes=mib * MIB)


def fwd_kernel(
    place, raw_0, raw_1, scale, offset, w_late, act_t, slope, late, sums, acts
):
    image = pl.program_id(0)
    now, before = acts.at[image % 2], acts.at[(image + 1) % 2]
    per = w_late.shape[0] // w_late.shape[1]
    for n in range(0, w_late.shape[1], 256):
        for c in range(per * n, per * (n + 256), 256):
            at = slice(c, c + 256)
            value = jnp.where(image < 4, raw_0[:, at], raw_1[:, at]).astype(F32)
            pre = value * scale[:, at] + offset[:, at]
            sig = sigmoid(pre)
            act = pre * sig
            slope[:, at] = (sig + act * (1.0 - sig)).astype(BF)
            act = act.astype(BF)
            now[:, at] = act
            turned = act.T
            for s in (0, 128):
                act_t[
                    pl.ds(pl.multiple_of(place[(c + s) // 128] * 128, 128), 128), :
                ] = turned[s : s + 128]
        at = slice(n, n + 256)
        value = jnp.dot(before[...], w_late[:, at], preferred_element_type=F32)
        one = jnp.sum(value, 0, keepdims=True)
        two = jnp.sum(value * value, 0, keepdims=True)
        level = jnp.where(image <= 1, one / value.shape[0], sums[2:3, at])
        late[:, at] = (value - level).astype(BF)
        sums[0:1, at] = jnp.where(image <= 1, 0.0, sums[0:1, at]) + one
        sums[1:2, at] = jnp.where(image <= 1, 0.0, sums[1:2, at]) + two
        sums[2:3, at] = level


def fwd_pass(place, raws, scale, offset, w_late):
    mid, out = w_late.shape
    rows = 2 * raws[0].shape[0]

    def current(i):
        return jnp.minimum(i, 7)

    return pl.pallas_call(
        fwd_kernel,
        out_shape=(
            jax.ShapeDtypeStruct((mid, rows), BF),
            jax.ShapeDtypeStruct((rows, mid), BF),
            jax.ShapeDtypeStruct((rows, out), BF),
            jax.ShapeDtypeStruct((8, out), F32),
        ),
        grid_spec=pltpu.PrefetchScalarGridSpec(
            num_scalar_prefetch=1,
            grid=(9,),
            in_specs=[
                pl.BlockSpec((256, mid), lambda i, p: (jnp.minimum(i, 3), 0)),
                pl.BlockSpec((256, mid), lambda i, p: (jnp.maximum(current(i) - 4, 0), 0)),
                pl.BlockSpec((1, mid), lambda i, p: (0, 0)),
                pl.BlockSpec((1, mid), lambda i, p: (0, 0)),
                pl.BlockSpec(memory_space=pltpu.VMEM),
            ],
            out_specs=[
                pl.BlockSpec((mid, 256), lambda i, p: (0, current(i))),
                pl.BlockSpec((256, mid), lambda i, p: (current(i), 0)),
                pl.BlockSpec((256, out), lambda i, p: (jnp.maximum(i - 1, 0), 0)),
                pl.BlockSpec((8, out), lambda i, p: (0, 0)),
            ],
            scratch_shapes=[pltpu.VMEM((2, 256, mid), BF)],
        ),
        cost_estimate=pl.CostEstimate(
            flops=2 * rows * mid * out,
            bytes_accessed=rows * (mid * 6 + out * 2) + 2 * mid * out,
            transcendentals=rows * mid,
        ),
        compiler_params=params(LIMIT),
    )(place, *raws, scale, offset, w_late)


def late_kernel(order, late, cot, scale, offset, out, grad, sums):
    @pl.when(pl.program_id(0) == 0)
    def _():
        sums[...] = jnp.zeros_like(sums)

    def step(k, carry):
        one, two = carry
        at = pl.ds(pl.multiple_of(k * 16, 16), 16)
        value = late[at, :].astype(F32)
        pre = value * scale[...] + offset[...]
        sig = sigmoid(pre)
        gate = pre * sig
        out[0, at, :] = gate.astype(BF)
        grad_y = cot[0, at, :].astype(F32) * (sig + gate * (1.0 - sig))
        grad[at, :] = grad_y.astype(BF)
        both = grad_y * value
        return one + grad_y[:8] + grad_y[8:], two + both[:8] + both[8:]

    zero = jnp.zeros((8, late.shape[1]), F32)
    one, two = lax.fori_loop(0, late.shape[0] // 16, step, (zero, zero), unroll=2)
    sums[0:1] += jnp.sum(one, 0, keepdims=True)
    sums[1:2] += jnp.sum(two, 0, keepdims=True)


def late_pass(order, late, cot, scale, offset):
    rows, width = late.shape
    vector = pl.BlockSpec((1, width), lambda i, o: (0, 0))
    return pl.pallas_call(
        late_kernel,
        out_shape=(
            jax.ShapeDtypeStruct(cot.shape, BF),
            jax.ShapeDtypeStruct((rows, width), BF),
            jax.ShapeDtypeStruct((8, width), F32),
        ),
        grid_spec=pltpu.PrefetchScalarGridSpec(
            num_scalar_prefetch=1,
            grid=(rows // 256,),
            in_specs=[
                pl.BlockSpec((256, width), lambda i, o: (i, 0)),
                pl.BlockSpec((1, 256, width), lambda i, o: (o[i], 0, 0)),
                vector,
                vector,
            ],
            out_specs=[
                pl.BlockSpec((1, 256, width), lambda i, o: (o[i], 0, 0)),
                pl.BlockSpec((256, width), lambda i, o: (i, 0)),
                pl.BlockSpec((8, width), lambda i, o: (0, 0)),
            ],
        ),
        cost_estimate=pl.CostEstimate(
            flops=16 * rows * width, bytes_accessed=rows * width * 8, transcendentals=rows * width
        ),
        compiler_params=params(LIMIT),
    )(order, late, cot, scale[None], offset[None])


def weight_kernel(turned, grad_h, out):
    for n in range(0, out.shape[1], 256):
        out[:, n : n + 256] = jnp.dot(
            turned[...], grad_h[:, n : n + 256], preferred_element_type=F32
        ).astype(BF)


def weight_grad(turned, grad_h):
    depth, rows = turned.shape
    width = grad_h.shape[1]
    return pl.pallas_call(
        weight_kernel,
        grid=(depth // 512,),
        out_shape=jax.ShapeDtypeStruct((depth, width), BF),
        in_specs=[
            pl.BlockSpec((512, rows), lambda i: (i, 0)),
            pl.BlockSpec(memory_space=pltpu.VMEM),
        ],
        out_specs=pl.BlockSpec((512, width), lambda i: (i, 0)),
        cost_estimate=pl.CostEstimate(
            flops=2 * depth * rows * width,
            bytes_accessed=2 * (depth * rows + rows * width + depth * width),
            transcendentals=0,
        ),
        compiler_params=params(LIMIT),
    )(turned, grad_h)


def early_kernel(
    grad_h, turned_0, turned_1, raw_0, raw_1, slope, w_late, term, grad_pre
):
    depth, cut = turned_0.shape
    one = two = 0.0
    for r in range(0, grad_h.shape[0], 512):
        at = slice(r, r + 512)
        grad = lax.dot_general(
            grad_h[at, :], w_late[...], (((1,), (1,)), ((), ())), preferred_element_type=F32
        )
        grad = grad * slope[at, :].astype(F32)
        one += jnp.sum(grad, 0, keepdims=True)
        raw = (raw_0 if r < cut else raw_1)[r % cut : r % cut + 512, :]
        two += jnp.sum(grad * raw.astype(F32), 0, keepdims=True)
        grad_pre[at, :] = grad.astype(BF)
    one_high, two_high = one.astype(BF), two.astype(BF)
    term[depth : depth + 16, :] = jnp.concatenate(
        [
            one_high,
            two_high,
            (one - one_high.astype(F32)).astype(BF),
            (two - two_high.astype(F32)).astype(BF),
            jnp.zeros((12, term.shape[1]), BF),
        ],
        0,
    )
    for m in range(0, depth, 512):
        term[m : m + 512, :] = (
            jnp.dot(turned_0[m : m + 512, :], grad_pre[:cut, :], preferred_element_type=F32)
            + jnp.dot(turned_1[m : m + 512, :], grad_pre[cut:, :], preferred_element_type=F32)
        ).astype(BF)


def early_grad(grad_h, turned, w_late, slope, raws, first, width):
    rows, out = grad_h.shape
    depth = turned[0].shape[0]
    tile = 256
    base = first // tile
    column = pl.BlockSpec((rows, tile), lambda j: (0, j + base))
    half = pl.BlockSpec((rows // 2, tile), lambda j: (0, j + base))
    return pl.pallas_call(
        early_kernel,
        grid=(width // tile,),
        out_shape=jax.ShapeDtypeStruct((depth + 16, width), BF),
        in_specs=[pl.BlockSpec(memory_space=pltpu.VMEM)] * 3
        + [half, half, column, pl.BlockSpec((tile, out), lambda j: (j + base, 0))],
        out_specs=pl.BlockSpec((depth + 16, tile), lambda j: (0, j)),
        scratch_shapes=[pltpu.VMEM((rows, tile), BF)],
        cost_estimate=pl.CostEstimate(
            flops=2 * rows * width * (out + depth),
            bytes_accessed=2 * (rows * out + rows * depth + 4 * rows * width),
            transcendentals=0,
        ),
        compiler_params=params(LIMIT),
    )(grad_h, *turned, *raws, slope, w_late)


def widen_kernel(value, out):
    out[...] = value[...].astype(F32)


def widen_rows(value):
    rows, width = value.shape
    return pl.pallas_call(
        widen_kernel,
        grid=(8,),
        out_shape=jax.ShapeDtypeStruct((rows, width), F32),
        in_specs=[pl.BlockSpec((256, width), lambda i: (i, 0))],
        out_specs=pl.BlockSpec((256, width), lambda i: (i, 0)),
        cost_estimate=pl.CostEstimate(flops=0, bytes_accessed=rows * width * 6, transcendentals=0),
        compiler_params=params(8),
    )(value)


def pack_sums(sums):
    high = lax.reduce_precision(sums, 8, 7)
    rows = jnp.concatenate([high, sums - high], 0).astype(BF)
    return jnp.pad(rows, ((0, 12), (0, 0)))


def unpack_sums(rows):
    return rows[0:2].astype(F32) + rows[2:4].astype(F32)


def scatter_pair_sums(value, axis):
    half = (value.shape[0] - 16) // 2
    other = swap(value[half:], axis)
    total = value[:half].astype(F32) + other[:half].astype(F32)
    return total.astype(BF), unpack_sums(value[2 * half :]) + unpack_sums(other[half:])


def scatter_ring_sums(value, sums, axis):
    rows = value.shape[0] // 4
    packed = pack_sums(sums)
    one, two, three = (
        shift(jnp.concatenate([value[k * rows : (k + 1) * rows], packed], 0), axis, -k)
        for k in (1, 2, 3)
    )
    total = (value[:rows].astype(F32) + two[:rows].astype(F32)) + (
        one[:rows].astype(F32) + three[:rows].astype(F32)
    )
    return total, (sums + unpack_sums(two[rows:])) + (
        unpack_sums(one[rows:]) + unpack_sums(three[rows:])
    )


def body(images, w_early, gain_early, bias_early, w_late, gain_late, bias_late, cotangent):
    width_in, width_mid = w_early.shape
    width_out = w_late.shape[1]
    pixels = images.shape[3]
    own = images.reshape(pixels, width_in)
    chan = lax.axis_index("chan")
    batch = lax.axis_index("batch")
    section = lax.axis_index("section")
    x_pos, z_pos = chan // 2, chan % 2
    y_pos, core = batch // 2, batch % 2
    count = float(pixels * 64)

    at = jnp.arange(width_in, dtype=jnp.int32)
    p_core, p_x, p_z = at // 512, (at // 128) % 4, (at // 64) % 2
    p_y, p_sec, p_row = (at // 16) % 4, (at // 8) % 2, at % 8
    source = (
        (p_sec ^ section) * 512
        + (((p_x + x_pos) % 4) * 2 + (p_z ^ z_pos)) * 64
        + (((p_y + y_pos) % 4) * 2 + (p_core ^ core)) * 8
        + p_row
    )
    (pick,) = tie((source[:, None] == at[None, :]).astype(BF))

    def turn(rows):
        return lax.dot_general(
            pick, rows, (((1,), (1,)), ((), ())), preferred_element_type=F32
        ).astype(BF)

    def products(turned, raw):
        here = turned.reshape(2, 512, -1)[:, :64].reshape(128, -1)
        cross = jnp.dot(here, raw, preferred_element_type=F32)
        return cross, jnp.sum(here.astype(F32), 1)

    def early(rows):
        return jnp.dot(rows, w_early, preferred_element_type=F32).astype(BF)

    half = pixels // 2
    deep = swap(own, "chan")
    right = shift(own, "chan", 1)
    left = shift(own, "chan", 3)
    raw_own = jnp.dot(own, w_early, preferred_element_type=F32)
    sums_e = jnp.stack([jnp.sum(raw_own, 0), jnp.sum(raw_own * raw_own, 0)])
    sums_e, deep, right, left = tie(sum_pair(sums_e, "batch"), deep, right, left)
    far_0 = shift(right[:half], "chan", 1)
    far_1 = shift(left[half:], "chan", 3)
    near = jnp.concatenate([own, right, left, deep], 0)
    raw_0 = early(near)
    sums_e = sum_ring(sums_e, "batch")
    sums_e, far_0, far_1, deep, raw_0 = tie(sums_e, far_0, far_1, deep, raw_0)
    sums_e = sum_ring(sums_e, "chan")
    deep_right = shift(deep, "chan", 1)
    deep_left = shift(deep, "chan", 3)
    deep_far = swap(jnp.concatenate([far_0, far_1], 0), "chan")
    sums_e = sum_pair(sums_e, "chan")
    sums_e, raw_0, near, *rest = tie(
        sums_e, raw_0, near, far_0, far_1, deep_right, deep_left, deep_far
    )
    mean_e = sums_e[0] / count
    rstd_e = lax.rsqrt(sums_e[1] / count - mean_e * mean_e + 1e-05)
    scale_e = rstd_e * gain_early
    offset_e = bias_early - mean_e * scale_e

    order = jnp.stack(
        [
            ((x_pos + dx) % 4) * 2 + (z_pos ^ dz)
            for dx, dz in ((0, 0), (1, 0), (3, 0), (0, 1), (2, 0), (1, 1), (3, 1), (2, 1))
        ]
    ).astype(jnp.int32)

    place = jnp.arange(16, dtype=jnp.int32)
    rest = jnp.concatenate(rest, 0)
    raws = [raw_0, early(rest)]
    act_t, slope, late, sums_l = fwd_pass(
        place, raws, scale_e[None], offset_e[None], w_late
    )
    level = sums_l[2]
    sums_l = sum_pair(sums_l[:2], "batch")
    sums_l, rest, near = tie(sums_l, rest, near)
    turned = [turn(near), turn(rest)]
    sums_l = sum_ring(sums_l, "batch") / count
    sums_l, *turned = tie(sums_l, *turned)
    mean_l = sums_l[0]
    rstd_l = lax.rsqrt(sums_l[1] - mean_l * mean_l + 1e-05)
    near_l = mean_l - level
    scale_l = rstd_l * gain_late
    offset_l = bias_late - near_l * scale_l
    late_out, grad_y, back = late_pass(
        order, late, cotangent.reshape(8, pixels, width_out), scale_l, offset_l
    )
    late_out = late_out.reshape(cotangent.shape)

    back = jnp.stack([back[0], back[1] + level * back[0]])
    back = sum_pair(back, "batch")
    back, *turned = tie(back, *turned)
    cross, colsum = products(turned[0], raws[0])
    more, columns = products(turned[1], raws[1])
    cross, colsum = cross + more, colsum + columns
    back = sum_ring(back, "batch") / count
    back, cross, colsum = tie(back, cross, colsum)
    back_one = back[0]
    back_two = rstd_l * (back[1] - mean_l * back_one)
    by_late = -scale_l * rstd_l * back_two
    constant = -scale_l * back_one - near_l * by_late

    grad_h = (grad_y.astype(F32) * scale_l + late.astype(F32) * by_late + constant).astype(BF)
    (grad_h,) = tie(grad_h)

    late = weight_grad(act_t, grad_h)
    cross = jnp.concatenate([cross, jnp.broadcast_to(colsum[:, None], (128, 128))], 1)
    cross = scatter_pair(cross, "batch")
    grad_h, late, cross = tie(grad_h, late, cross)
    late = lax.psum_scatter(late, "batch", tiled=True)
    step = width_mid // 2

    def early_cut(k, grad_h):
        return early_grad(grad_h, turned, w_late, slope, raws, k * step, step)

    term_a = early_cut(0, grad_h)
    cross = scatter_ring(cross, "batch")
    grad_h, term_a, cross = tie(grad_h, term_a, cross)
    part_a, sums_a = scatter_pair_sums(term_a, "batch")
    term_b = early_cut(1, grad_h)
    term_b, part_a, sums_a, late = tie(term_b, part_a, sums_a, late)
    late = sum_pair(late, "section")
    part_a, sums_a = scatter_ring_sums(part_a, sums_a, "chan")
    part_b, sums_b = scatter_pair_sums(term_b, "batch")
    part_a, sums_a, part_b, sums_b, late = tie(part_a, sums_a, part_b, sums_b, late)
    late = lax.all_gather(late, "batch", tiled=True)
    part_b, sums_b = scatter_ring_sums(part_b, sums_b, "chan")
    grad = jnp.concatenate([part_a, part_b], 1).astype(BF)
    sums_g = jnp.concatenate([sums_a, sums_b], 1)
    grad, sums_g = scatter_pair_sums(jnp.concatenate([grad, pack_sums(sums_g)], 0), "chan")
    grad = grad.astype(F32)
    grad_late = widen_rows(late)
    colsum = cross[:, width_mid:][:, :1]
    cross = rstd_e * (cross[:, :width_mid] - colsum * mean_e)
    parts = [
        jnp.concatenate([grad[k * 16 : (k + 1) * 16], sums_g], 0) for k in range(4)
    ]
    one, two, three = (shift(parts[k], "batch", -k) for k in (1, 2, 3))
    total = (parts[0] + two) + (one + three)
    grad, sums_g = total[:16], total[16:] / count
    back_one = sums_g[:1]
    back_two = rstd_e * (sums_g[1:] - mean_e * back_one)
    grad = scale_e * (grad - colsum * back_one - cross * back_two)
    grad_early = scatter_pair(grad, "section")
    return (late_out, grad_late, grad_early)


def solution(mesh):
    return jax.shard_map(
        body,
        mesh=mesh,
        in_specs=(
            P("section", "batch", "chan", None, None),
            P(),
            P(),
            P(),
            P(None, "chan"),
            P("chan"),
            P("chan"),
            P("section", "batch", None, "chan"),
        ),
        out_specs=(
            P("section", "batch", None, "chan"),
            P(None, "chan"),
            P(("section", "chan", "batch"), None),
        ),
        check_vma=False,
    )
```

```python
import functools

import jax
import jax.numpy as jnp
from jax import lax
from jax.experimental import pallas as pl
from jax.experimental.pallas import tpu as pltpu
from jax.sharding import PartitionSpec as P

BF = jnp.bfloat16
F32 = jnp.float32
MIB = 1 << 20


def shift(value, axis, step):
    return lax.ppermute(
        value, axis, [(i, ((i // 2 - step) % 4) * 2 + i % 2) for i in range(8)]
    )


def swap(value, axis):
    size = 2 if axis == "section" else 8
    return lax.ppermute(value, axis, [(i, i ^ 1) for i in range(size)])


def sum_pair(value, axis):
    return value + swap(value, axis)


def sum_ring(value, axis):
    one, two, three = (shift(value, axis, step) for step in (1, 2, 3))
    return (value + two) + (one + three)


def sum_batch(value):
    return sum_ring(sum_pair(value, "batch"), "batch")


def scatter_pair(value, axis):
    rows = value.shape[0] // 2
    return value[:rows].astype(F32) + swap(value[rows:], axis).astype(F32)


def scatter_ring(value, axis):
    rows = value.shape[0] // 4
    one, two, three = (
        shift(value[k * rows : (k + 1) * rows], axis, -k).astype(F32) for k in (1, 2, 3)
    )
    return (value[:rows].astype(F32) + two) + (one + three)


def tie(*values):
    return lax.optimization_barrier(values)


def sigmoid(value):
    return 0.5 * jnp.tanh(0.5 * value) + 0.5


def params(mib):
    return pltpu.CompilerParams(vmem_limit_bytes=mib * MIB)


def fwd_kernel(
    raw_0, raw_1, scale, offset, w_late, act_t, slope, late, sums, acts
):
    image = pl.program_id(0)
    for c in range(0, w_late.shape[0], 256):
        at = slice(c, c + 256)
        value = jnp.where(image < 4, raw_0[:, at], raw_1[:, at]).astype(F32)
        pre = (value * scale[:, at] + offset[:, at]).astype(BF)
        sig = sigmoid(pre)
        act = pre * sig
        slope[:, at] = sig + act * (1.0 - sig)
        acts[:, at] = act
        act_t[at, :] = act.T
    for n in range(0, w_late.shape[1], 256):
        at = slice(n, n + 256)
        value = jnp.dot(acts[...], w_late[:, at], preferred_element_type=F32)
        one = jnp.sum(value, 0, keepdims=True)
        two = jnp.sum(value * value, 0, keepdims=True)
        level = jnp.where(image == 0, one / value.shape[0], sums[2:3, at])
        late[:, at] = (value - level).astype(BF)
        sums[0:1, at] = jnp.where(image == 0, 0.0, sums[0:1, at]) + one
        sums[1:2, at] = jnp.where(image == 0, 0.0, sums[1:2, at]) + two
        sums[2:3, at] = level


def fwd_pass(raws, scale, offset, w_late):
    mid, out = w_late.shape
    rows = 2 * raws[0].shape[0]

    return pl.pallas_call(
        fwd_kernel,
        out_shape=(
            jax.ShapeDtypeStruct((mid, rows), BF),
            jax.ShapeDtypeStruct((rows, mid), BF),
            jax.ShapeDtypeStruct((rows, out), BF),
            jax.ShapeDtypeStruct((8, out), F32),
        ),
        grid_spec=pl.GridSpec(
            grid=(8,),
            in_specs=[
                pl.BlockSpec((256, mid), lambda i: (jnp.minimum(i, 3), 0)),
                pl.BlockSpec((256, mid), lambda i: (jnp.maximum(i - 4, 0), 0)),
                pl.BlockSpec((1, mid), lambda i: (0, 0)),
                pl.BlockSpec((1, mid), lambda i: (0, 0)),
                pl.BlockSpec(memory_space=pltpu.VMEM),
            ],
            out_specs=[
                pl.BlockSpec((mid, 256), lambda i: (0, i)),
                pl.BlockSpec((256, mid), lambda i: (i, 0)),
                pl.BlockSpec((256, out), lambda i: (i, 0)),
                pl.BlockSpec((8, out), lambda i: (0, 0)),
            ],
            scratch_shapes=[pltpu.VMEM((256, mid), BF)],
        ),
        cost_estimate=pl.CostEstimate(
            flops=2 * rows * mid * out,
            bytes_accessed=rows * (mid * 6 + out * 2) + 2 * mid * out,
            transcendentals=rows * mid,
        ),
        compiler_params=params(52),
    )(*raws, scale, offset, w_late)


def late_kernel(order, late, cot, scale, offset, out, grad, sums):
    @pl.when(pl.program_id(0) == 0)
    def _():
        sums[...] = jnp.zeros_like(sums)

    def step(k, carry):
        one, two = carry
        at = pl.ds(pl.multiple_of(k * 16, 16), 16)
        value = late[at, :].astype(F32)
        pre = value * scale[...] + offset[...]
        sig = sigmoid(pre)
        gate = pre * sig
        out[0, at, :] = gate.astype(BF)
        grad_y = cot[0, at, :].astype(F32) * (sig + gate * (1.0 - sig))
        grad[at, :] = grad_y.astype(BF)
        both = grad_y * value
        return one + grad_y[:8] + grad_y[8:], two + both[:8] + both[8:]

    zero = jnp.zeros((8, late.shape[1]), F32)
    one, two = lax.fori_loop(0, late.shape[0] // 16, step, (zero, zero), unroll=2)
    sums[0:1] += jnp.sum(one, 0, keepdims=True)
    sums[1:2] += jnp.sum(two, 0, keepdims=True)


def late_pass(order, late, cot, scale, offset):
    rows, width = late.shape
    vector = pl.BlockSpec((1, width), lambda i, o: (0, 0))
    return pl.pallas_call(
        late_kernel,
        out_shape=(
            jax.ShapeDtypeStruct(cot.shape, BF),
            jax.ShapeDtypeStruct((rows, width), BF),
            jax.ShapeDtypeStruct((8, width), F32),
        ),
        grid_spec=pltpu.PrefetchScalarGridSpec(
            num_scalar_prefetch=1,
            grid=(rows // 256,),
            in_specs=[
                pl.BlockSpec((256, width), lambda i, o: (i, 0)),
                pl.BlockSpec((1, 256, width), lambda i, o: (o[i], 0, 0)),
                vector,
                vector,
            ],
            out_specs=[
                pl.BlockSpec((1, 256, width), lambda i, o: (o[i], 0, 0)),
                pl.BlockSpec((256, width), lambda i, o: (i, 0)),
                pl.BlockSpec((8, width), lambda i, o: (0, 0)),
            ],
        ),
        cost_estimate=pl.CostEstimate(
            flops=16 * rows * width, bytes_accessed=rows * width * 8, transcendentals=rows * width
        ),
        compiler_params=params(24),
    )(order, late, cot, scale[None], offset[None])


def weight_kernel(turned, grad_h, out):
    for n in range(0, out.shape[1], 256):
        out[:, n : n + 256] = jnp.dot(
            turned[...], grad_h[:, n : n + 256], preferred_element_type=F32
        ).astype(BF)


def weight_grad(turned, grad_h):
    depth, rows = turned.shape
    width = grad_h.shape[1]
    return pl.pallas_call(
        weight_kernel,
        grid=(depth // 512,),
        out_shape=jax.ShapeDtypeStruct((depth, width), BF),
        in_specs=[
            pl.BlockSpec((512, rows), lambda i: (i, 0)),
            pl.BlockSpec(memory_space=pltpu.VMEM),
        ],
        out_specs=pl.BlockSpec((512, width), lambda i: (i, 0)),
        cost_estimate=pl.CostEstimate(
            flops=2 * depth * rows * width,
            bytes_accessed=2 * (depth * rows + rows * width + depth * width),
            transcendentals=0,
        ),
        compiler_params=params(40),
    )(turned, grad_h)


def early_kernel(
    grad_h, turned_0, turned_1, raw_0, raw_1, slope, w_late, term, grad_pre
):
    depth, cut = turned_0.shape
    one = two = 0.0
    for r in range(0, grad_h.shape[0], 512):
        at = slice(r, r + 512)
        grad = lax.dot_general(
            grad_h[at, :], w_late[...], (((1,), (1,)), ((), ())), preferred_element_type=F32
        )
        grad = grad * slope[at, :].astype(F32)
        one += jnp.sum(grad, 0, keepdims=True)
        raw = (raw_0 if r < cut else raw_1)[r % cut : r % cut + 512, :]
        two += jnp.sum(grad * raw.astype(F32), 0, keepdims=True)
        grad_pre[at, :] = grad.astype(BF)
    one_high, two_high = one.astype(BF), two.astype(BF)
    term[depth : depth + 16, :] = jnp.concatenate(
        [
            one_high,
            two_high,
            (one - one_high.astype(F32)).astype(BF),
            (two - two_high.astype(F32)).astype(BF),
            jnp.zeros((12, term.shape[1]), BF),
        ],
        0,
    )
    for m in range(0, depth, 512):
        term[m : m + 512, :] = (
            jnp.dot(turned_0[m : m + 512, :], grad_pre[:cut, :], preferred_element_type=F32)
            + jnp.dot(turned_1[m : m + 512, :], grad_pre[cut:, :], preferred_element_type=F32)
        ).astype(BF)


def early_grad(grad_h, turned, w_late, slope, raws, first, width):
    rows, out = grad_h.shape
    depth = turned[0].shape[0]
    tile = 256
    base = first // tile
    column = pl.BlockSpec((rows, tile), lambda j: (0, j + base))
    half = pl.BlockSpec((rows // 2, tile), lambda j: (0, j + base))
    return pl.pallas_call(
        early_kernel,
        grid=(width // tile,),
        out_shape=jax.ShapeDtypeStruct((depth + 16, width), BF),
        in_specs=[pl.BlockSpec(memory_space=pltpu.VMEM)] * 3
        + [half, half, column, pl.BlockSpec((tile, out), lambda j: (j + base, 0))],
        out_specs=pl.BlockSpec((depth + 16, tile), lambda j: (0, j)),
        scratch_shapes=[pltpu.VMEM((rows, tile), BF)],
        cost_estimate=pl.CostEstimate(
            flops=2 * rows * width * (out + depth),
            bytes_accessed=2 * (rows * out + rows * depth + 4 * rows * width),
            transcendentals=0,
        ),
        compiler_params=params(40),
    )(grad_h, *turned, *raws, slope, w_late)


def widen_kernel(value, out):
    out[...] = value[...].astype(F32)


def widen_rows(value):
    rows, width = value.shape
    return pl.pallas_call(
        widen_kernel,
        grid=(8,),
        out_shape=jax.ShapeDtypeStruct((rows, width), F32),
        in_specs=[pl.BlockSpec((256, width), lambda i: (i, 0))],
        out_specs=pl.BlockSpec((256, width), lambda i: (i, 0)),
        cost_estimate=pl.CostEstimate(flops=0, bytes_accessed=rows * width * 6, transcendentals=0),
        compiler_params=params(56),
    )(value)


def pack_sums(sums):
    high = lax.reduce_precision(sums, 8, 7)
    rows = jnp.concatenate([high, sums - high], 0).astype(BF)
    return jnp.pad(rows, ((0, 12), (0, 0)))


def unpack_sums(rows):
    return rows[0:2].astype(F32) + rows[2:4].astype(F32)


def scatter_pair_sums(value, axis):
    half = (value.shape[0] - 16) // 2
    other = swap(value[half:], axis)
    total = value[:half].astype(F32) + other[:half].astype(F32)
    return total.astype(BF), unpack_sums(value[2 * half :]) + unpack_sums(other[half:])


def ring_messages(value, sums, axis):
    rows = value.shape[0] // 4
    packed = pack_sums(sums)
    return [
        shift(jnp.concatenate([value[k * rows : (k + 1) * rows], packed], 0), axis, -k)
        for k in (1, 2, 3)
    ]


def ring_total(value, sums, one, two, three):
    rows = value.shape[0] // 4
    total = (value[:rows].astype(F32) + two[:rows].astype(F32)) + (
        one[:rows].astype(F32) + three[:rows].astype(F32)
    )
    return total, (sums + unpack_sums(two[rows:])) + (
        unpack_sums(one[rows:]) + unpack_sums(three[rows:])
    )


def body(images, w_early, gain_early, bias_early, w_late, gain_late, bias_late, cotangent):
    width_in, width_mid = w_early.shape
    width_out = w_late.shape[1]
    pixels = images.shape[3]
    own = images.reshape(pixels, width_in)
    chan = lax.axis_index("chan")
    batch = lax.axis_index("batch")
    section = lax.axis_index("section")
    x_pos, z_pos = chan // 2, chan % 2
    y_pos, core = batch // 2, batch % 2
    count = float(pixels * 64)

    at = jnp.arange(width_in, dtype=jnp.int32)
    p_core, p_x, p_z = at // 512, (at // 128) % 4, (at // 64) % 2
    p_y, p_sec, p_row = (at // 16) % 4, (at // 8) % 2, at % 8
    source = (
        (p_sec ^ section) * 512
        + (((p_x + x_pos) % 4) * 2 + (p_z ^ z_pos)) * 64
        + (((p_y + y_pos) % 4) * 2 + (p_core ^ core)) * 8
        + p_row
    )
    (pick,) = tie((source[:, None] == at[None, :]).astype(BF))

    def turn(rows):
        return lax.dot_general(
            pick, rows, (((1,), (1,)), ((), ())), preferred_element_type=F32
        ).astype(BF)

    def products(turned, raw):
        here = turned.reshape(2, 512, -1)[:, :64].reshape(128, -1)
        cross = jnp.dot(here, raw, preferred_element_type=F32)
        return cross, jnp.sum(here.astype(F32), 1)

    def early(rows):
        return jnp.dot(rows, w_early, preferred_element_type=F32).astype(BF)

    half = pixels // 2
    deep = swap(own, "chan")
    right = shift(own, "chan", 1)
    left = shift(own, "chan", 3)
    raw_own = jnp.dot(own, w_early, preferred_element_type=F32)
    sums_e = jnp.stack([jnp.sum(raw_own, 0), jnp.sum(raw_own * raw_own, 0)])
    sums_e, deep, right, left = tie(sum_pair(sums_e, "batch"), deep, right, left)
    far_0 = shift(right[:half], "chan", 1)
    far_1 = shift(left[half:], "chan", 3)
    near = jnp.concatenate([own, right, left, deep], 0)
    raw_0 = early(near)
    sums_e = sum_ring(sums_e, "batch")
    sums_e, far_0, far_1, deep, raw_0 = tie(sums_e, far_0, far_1, deep, raw_0)
    sums_e = sum_ring(sum_pair(sums_e, "chan"), "chan")
    deep_right = shift(deep, "chan", 1)
    deep_left = shift(deep, "chan", 3)
    deep_far = swap(jnp.concatenate([far_0, far_1], 0), "chan")
    sums_e, raw_0, near, *rest = tie(
        sums_e, raw_0, near, far_0, far_1, deep_right, deep_left, deep_far
    )
    mean_e = sums_e[0] / count
    rstd_e = lax.rsqrt(sums_e[1] / count - mean_e * mean_e + 1e-05)
    scale_e = rstd_e * gain_early
    offset_e = bias_early - mean_e * scale_e

    order = jnp.stack(
        [
            ((x_pos + dx) % 4) * 2 + (z_pos ^ dz)
            for dx, dz in ((0, 0), (1, 0), (3, 0), (0, 1), (2, 0), (1, 1), (3, 1), (2, 1))
        ]
    ).astype(jnp.int32)

    rest = jnp.concatenate(rest, 0)
    raws = [raw_0, early(rest)]
    act_t, slope, late, sums_l = fwd_pass(
        raws, scale_e[None], offset_e[None], w_late
    )
    level = sums_l[2]
    sums_l = sum_pair(sums_l[:2], "batch")
    sums_l, rest, near = tie(sums_l, rest, near)
    turned = [turn(near), turn(rest)]
    sums_l = sum_ring(sums_l, "batch") / count
    sums_l, *turned = tie(sums_l, *turned)
    mean_l = sums_l[0]
    rstd_l = lax.rsqrt(sums_l[1] - mean_l * mean_l + 1e-05)
    near_l = mean_l - level
    scale_l = rstd_l * gain_late
    offset_l = bias_late - near_l * scale_l
    late_out, grad_y, back = late_pass(
        order, late, cotangent.reshape(8, pixels, width_out), scale_l, offset_l
    )
    late_out = late_out.reshape(cotangent.shape)

    back = jnp.stack([back[0], back[1] + level * back[0]])
    back = sum_pair(back, "batch")
    back, *turned = tie(back, *turned)
    cross, colsum = products(turned[0], raws[0])
    more, columns = products(turned[1], raws[1])
    cross, colsum = cross + more, colsum + columns
    back = sum_ring(back, "batch") / count
    back, cross, colsum = tie(back, cross, colsum)
    back_one = back[0]
    back_two = rstd_l * (back[1] - mean_l * back_one)
    by_late = -scale_l * rstd_l * back_two
    constant = -scale_l * back_one - near_l * by_late

    grad_h = (grad_y.astype(F32) * scale_l + late.astype(F32) * by_late + constant).astype(BF)
    (grad_h,) = tie(grad_h)

    late = weight_grad(act_t, grad_h)
    grad_h, late, cross = tie(grad_h, late, cross)
    late = lax.psum_scatter(late, "batch", tiled=True)
    step = width_mid // 2

    def early_cut(k, grad_h):
        return early_grad(grad_h, turned, w_late, slope, raws, k * step, step)

    term_a = early_cut(0, grad_h)
    grad_h, term_a = tie(grad_h, term_a)
    part_a, sums_a = scatter_pair_sums(term_a, "batch")
    term_b = early_cut(1, grad_h)
    term_b, part_a, sums_a = tie(term_b, part_a, sums_a)
    part_b, sums_b = scatter_pair_sums(term_b, "batch")
    part_a, sums_a, part_b, sums_b, late = tie(part_a, sums_a, part_b, sums_b, late)
    grad = jnp.concatenate([part_a, part_b], 1)
    sums_g = jnp.concatenate([sums_a, sums_b], 1)
    one, two, three = ring_messages(grad, sums_g, "chan")
    late = sum_pair(late, "section")
    two, late = tie(two, late)
    late = lax.all_gather(late, "batch", tiled=True)
    cross = jnp.concatenate([cross, jnp.broadcast_to(colsum[:, None], (128, 128))], 1)
    cross = scatter_pair(cross, "batch")
    grad, sums_g = ring_total(grad, sums_g, one, two, three)
    grad, sums_g, cross = tie(grad, sums_g, cross)
    cross = scatter_ring(cross, "batch")
    grad = jnp.concatenate([grad.astype(BF), pack_sums(sums_g)], 0)
    grad, sums_g = scatter_pair_sums(grad, "chan")
    grad = grad.astype(F32)
    grad_late = widen_rows(late)
    colsum = cross[:, width_mid:][:, :1]
    cross = rstd_e * (cross[:, :width_mid] - colsum * mean_e)
    parts = [
        jnp.concatenate([grad[k * 16 : (k + 1) * 16], sums_g], 0) for k in range(4)
    ]
    one, two, three = (shift(parts[k], "batch", -k) for k in (1, 2, 3))
    one, two, three, grad_late = tie(one, two, three, grad_late)
    total = (parts[0] + two) + (one + three)
    grad, sums_g = total[:16], total[16:] / count
    back_one = sums_g[:1]
    back_two = rstd_e * (sums_g[1:] - mean_e * back_one)
    grad = scale_e * (grad - colsum * back_one - cross * back_two)
    grad_early = scatter_pair(grad, "section")
    return (late_out, grad_late, grad_early)


def solution(mesh):
    return jax.shard_map(
        body,
        mesh=mesh,
        in_specs=(
            P("section", "batch", "chan", None, None),
            P(),
            P(),
            P(),
            P(None, "chan"),
            P("chan"),
            P("chan"),
            P("section", "batch", None, "chan"),
        ),
        out_specs=(
            P("section", "batch", None, "chan"),
            P(None, "chan"),
            P(("section", "chan", "batch"), None),
        ),
        check_vma=False,
    )
```

```python
import functools

import jax
import jax.numpy as jnp
from jax import lax
from jax.experimental import pallas as pl
from jax.experimental.pallas import tpu as pltpu
from jax.sharding import PartitionSpec as P

BF = jnp.bfloat16
F32 = jnp.float32
MIB = 1 << 20


def shift(value, axis, step):
    return lax.ppermute(
        value, axis, [(i, ((i // 2 - step) % 4) * 2 + i % 2) for i in range(8)]
    )


def swap(value, axis):
    size = 2 if axis == "section" else 8
    return lax.ppermute(value, axis, [(i, i ^ 1) for i in range(size)])


def sum_pair(value, axis):
    return value + swap(value, axis)


def sum_ring(value, axis):
    one, two, three = (shift(value, axis, step) for step in (1, 2, 3))
    return (value + two) + (one + three)


def sum_batch(value):
    return sum_ring(sum_pair(value, "batch"), "batch")


def scatter_pair(value, axis):
    rows = value.shape[0] // 2
    return value[:rows].astype(F32) + swap(value[rows:], axis).astype(F32)


def scatter_ring(value, axis):
    rows = value.shape[0] // 4
    one, two, three = (
        shift(value[k * rows : (k + 1) * rows], axis, -k).astype(F32) for k in (1, 2, 3)
    )
    return (value[:rows].astype(F32) + two) + (one + three)


def tie(*values):
    return lax.optimization_barrier(values)


def sigmoid(value):
    return 0.5 * jnp.tanh(0.5 * value) + 0.5


def params(mib):
    return pltpu.CompilerParams(vmem_limit_bytes=mib * MIB)


def fwd_kernel(
    raw_0, raw_1, scale, offset, w_late, act_t, slope, late, sums, acts
):
    image = pl.program_id(0)
    for c in range(0, w_late.shape[0], 256):
        at = slice(c, c + 256)
        value = jnp.where(image < 4, raw_0[:, at], raw_1[:, at]).astype(F32)
        pre = (value * scale[:, at] + offset[:, at]).astype(BF)
        sig = sigmoid(pre)
        act = pre * sig
        slope[:, at] = sig + act * (1.0 - sig)
        acts[:, at] = act
        act_t[at, :] = act.T
    for n in range(0, w_late.shape[1], 256):
        at = slice(n, n + 256)
        value = jnp.dot(acts[...], w_late[:, at], preferred_element_type=F32)
        one = jnp.sum(value, 0, keepdims=True)
        two = jnp.sum(value * value, 0, keepdims=True)
        level = jnp.where(image == 0, one / value.shape[0], sums[2:3, at])
        late[:, at] = (value - level).astype(BF)
        sums[0:1, at] = jnp.where(image == 0, 0.0, sums[0:1, at]) + one
        sums[1:2, at] = jnp.where(image == 0, 0.0, sums[1:2, at]) + two
        sums[2:3, at] = level


def fwd_pass(raws, scale, offset, w_late):
    mid, out = w_late.shape
    rows = 2 * raws[0].shape[0]

    return pl.pallas_call(
        fwd_kernel,
        out_shape=(
            jax.ShapeDtypeStruct((mid, rows), BF),
            jax.ShapeDtypeStruct((rows, mid), BF),
            jax.ShapeDtypeStruct((rows, out), BF),
            jax.ShapeDtypeStruct((8, out), F32),
        ),
        grid_spec=pl.GridSpec(
            grid=(8,),
            in_specs=[
                pl.BlockSpec((256, mid), lambda i: (jnp.minimum(i, 3), 0)),
                pl.BlockSpec((256, mid), lambda i: (jnp.maximum(i - 4, 0), 0)),
                pl.BlockSpec((1, mid), lambda i: (0, 0)),
                pl.BlockSpec((1, mid), lambda i: (0, 0)),
                pl.BlockSpec(memory_space=pltpu.VMEM),
            ],
            out_specs=[
                pl.BlockSpec((mid, 256), lambda i: (0, i)),
                pl.BlockSpec((256, mid), lambda i: (i, 0)),
                pl.BlockSpec((256, out), lambda i: (i, 0)),
                pl.BlockSpec((8, out), lambda i: (0, 0)),
            ],
            scratch_shapes=[pltpu.VMEM((256, mid), BF)],
        ),
        cost_estimate=pl.CostEstimate(
            flops=2 * rows * mid * out,
            bytes_accessed=rows * (mid * 6 + out * 2) + 2 * mid * out,
            transcendentals=rows * mid,
        ),
        compiler_params=params(52),
    )(*raws, scale, offset, w_late)


def late_kernel(order, late, cot, scale, offset, out, grad, sums):
    @pl.when(pl.program_id(0) == 0)
    def _():
        sums[...] = jnp.zeros_like(sums)

    def step(k, carry):
        one, two = carry
        at = pl.ds(pl.multiple_of(k * 16, 16), 16)
        value = late[at, :].astype(F32)
        pre = value * scale[...] + offset[...]
        sig = sigmoid(pre)
        gate = pre * sig
        out[0, at, :] = gate.astype(BF)
        grad_y = cot[0, at, :].astype(F32) * (sig + gate * (1.0 - sig))
        grad[at, :] = grad_y.astype(BF)
        both = grad_y * value
        return one + grad_y[:8] + grad_y[8:], two + both[:8] + both[8:]

    zero = jnp.zeros((8, late.shape[1]), F32)
    one, two = lax.fori_loop(0, late.shape[0] // 16, step, (zero, zero), unroll=2)
    sums[0:1] += jnp.sum(one, 0, keepdims=True)
    sums[1:2] += jnp.sum(two, 0, keepdims=True)


def late_pass(order, late, cot, scale, offset):
    rows, width = late.shape
    vector = pl.BlockSpec((1, width), lambda i, o: (0, 0))
    return pl.pallas_call(
        late_kernel,
        out_shape=(
            jax.ShapeDtypeStruct(cot.shape, BF),
            jax.ShapeDtypeStruct((rows, width), BF),
            jax.ShapeDtypeStruct((8, width), F32),
        ),
        grid_spec=pltpu.PrefetchScalarGridSpec(
            num_scalar_prefetch=1,
            grid=(rows // 256,),
            in_specs=[
                pl.BlockSpec((256, width), lambda i, o: (i, 0)),
                pl.BlockSpec((1, 256, width), lambda i, o: (o[i], 0, 0)),
                vector,
                vector,
            ],
            out_specs=[
                pl.BlockSpec((1, 256, width), lambda i, o: (o[i], 0, 0)),
                pl.BlockSpec((256, width), lambda i, o: (i, 0)),
                pl.BlockSpec((8, width), lambda i, o: (0, 0)),
            ],
        ),
        cost_estimate=pl.CostEstimate(
            flops=16 * rows * width, bytes_accessed=rows * width * 8, transcendentals=rows * width
        ),
        compiler_params=params(24),
    )(order, late, cot, scale[None], offset[None])


def weight_kernel(turned, grad_h, out):
    for n in range(0, out.shape[1], 256):
        out[:, n : n + 256] = jnp.dot(
            turned[...], grad_h[:, n : n + 256], preferred_element_type=F32
        ).astype(BF)


def weight_grad(turned, grad_h):
    depth, rows = turned.shape
    width = grad_h.shape[1]
    return pl.pallas_call(
        weight_kernel,
        grid=(depth // 512,),
        out_shape=jax.ShapeDtypeStruct((depth, width), BF),
        in_specs=[
            pl.BlockSpec((512, rows), lambda i: (i, 0)),
            pl.BlockSpec(memory_space=pltpu.VMEM),
        ],
        out_specs=pl.BlockSpec((512, width), lambda i: (i, 0)),
        cost_estimate=pl.CostEstimate(
            flops=2 * depth * rows * width,
            bytes_accessed=2 * (depth * rows + rows * width + depth * width),
            transcendentals=0,
        ),
        compiler_params=params(40),
    )(turned, grad_h)


def early_kernel(
    grad_h, turned_0, turned_1, raw_0, raw_1, slope, w_late, term, grad_pre
):
    depth, cut = turned_0.shape
    one = two = 0.0
    for r in range(0, grad_h.shape[0], 512):
        at = slice(r, r + 512)
        grad = lax.dot_general(
            grad_h[at, :], w_late[...], (((1,), (1,)), ((), ())), preferred_element_type=F32
        )
        grad = grad * slope[at, :].astype(F32)
        one += jnp.sum(grad, 0, keepdims=True)
        raw = (raw_0 if r < cut else raw_1)[r % cut : r % cut + 512, :]
        two += jnp.sum(grad * raw.astype(F32), 0, keepdims=True)
        grad_pre[at, :] = grad.astype(BF)
    one_high, two_high = one.astype(BF), two.astype(BF)
    term[depth : depth + 16, :] = jnp.concatenate(
        [
            one_high,
            two_high,
            (one - one_high.astype(F32)).astype(BF),
            (two - two_high.astype(F32)).astype(BF),
            jnp.zeros((12, term.shape[1]), BF),
        ],
        0,
    )
    for m in range(0, depth, 512):
        term[m : m + 512, :] = (
            jnp.dot(turned_0[m : m + 512, :], grad_pre[:cut, :], preferred_element_type=F32)
            + jnp.dot(turned_1[m : m + 512, :], grad_pre[cut:, :], preferred_element_type=F32)
        ).astype(BF)


def early_grad(grad_h, turned, w_late, slope, raws, first, width):
    rows, out = grad_h.shape
    depth = turned[0].shape[0]
    tile = 256
    base = first // tile
    column = pl.BlockSpec((rows, tile), lambda j: (0, j + base))
    half = pl.BlockSpec((rows // 2, tile), lambda j: (0, j + base))
    return pl.pallas_call(
        early_kernel,
        grid=(width // tile,),
        out_shape=jax.ShapeDtypeStruct((depth + 16, width), BF),
        in_specs=[pl.BlockSpec(memory_space=pltpu.VMEM)] * 3
        + [half, half, column, pl.BlockSpec((tile, out), lambda j: (j + base, 0))],
        out_specs=pl.BlockSpec((depth + 16, tile), lambda j: (0, j)),
        scratch_shapes=[pltpu.VMEM((rows, tile), BF)],
        cost_estimate=pl.CostEstimate(
            flops=2 * rows * width * (out + depth),
            bytes_accessed=2 * (rows * out + rows * depth + 4 * rows * width),
            transcendentals=0,
        ),
        compiler_params=params(40),
    )(grad_h, *turned, *raws, slope, w_late)


def widen_kernel(value, out):
    out[...] = value[...].astype(F32)


def widen_rows(value):
    rows, width = value.shape
    return pl.pallas_call(
        widen_kernel,
        grid=(8,),
        out_shape=jax.ShapeDtypeStruct((rows, width), F32),
        in_specs=[pl.BlockSpec((256, width), lambda i: (i, 0))],
        out_specs=pl.BlockSpec((256, width), lambda i: (i, 0)),
        cost_estimate=pl.CostEstimate(flops=0, bytes_accessed=rows * width * 6, transcendentals=0),
        compiler_params=params(56),
    )(value)


def pack_sums(sums):
    high = lax.reduce_precision(sums, 8, 7)
    rows = jnp.concatenate([high, sums - high], 0).astype(BF)
    return jnp.pad(rows, ((0, 12), (0, 0)))


def unpack_sums(rows):
    return rows[0:2].astype(F32) + rows[2:4].astype(F32)


def scatter_pair_sums(value, axis):
    half = (value.shape[0] - 16) // 2
    other = swap(value[half:], axis)
    total = value[:half].astype(F32) + other[:half].astype(F32)
    return total.astype(BF), unpack_sums(value[2 * half :]) + unpack_sums(other[half:])


def ring_messages(value, sums):
    rows = value.shape[0] // 4
    packed = pack_sums(sums)
    return [
        jnp.concatenate([value[k * rows : (k + 1) * rows], packed], 0) for k in (1, 2, 3)
    ]


def ring_total(value, sums, one, two, three):
    rows = value.shape[0] // 4
    total = (value[:rows].astype(F32) + two[:rows].astype(F32)) + (
        one[:rows].astype(F32) + three[:rows].astype(F32)
    )
    return total, (sums + unpack_sums(two[rows:])) + (
        unpack_sums(one[rows:]) + unpack_sums(three[rows:])
    )


def body(images, w_early, gain_early, bias_early, w_late, gain_late, bias_late, cotangent):
    width_in, width_mid = w_early.shape
    width_out = w_late.shape[1]
    pixels = images.shape[3]
    own = images.reshape(pixels, width_in)
    chan = lax.axis_index("chan")
    batch = lax.axis_index("batch")
    section = lax.axis_index("section")
    x_pos, z_pos = chan // 2, chan % 2
    y_pos, core = batch // 2, batch % 2
    count = float(pixels * 64)

    at = jnp.arange(width_in, dtype=jnp.int32)
    p_core, p_x, p_z = at // 512, (at // 128) % 4, (at // 64) % 2
    p_y, p_sec, p_row = (at // 16) % 4, (at // 8) % 2, at % 8
    source = (
        (p_sec ^ section) * 512
        + (((p_x + x_pos) % 4) * 2 + (p_z ^ z_pos)) * 64
        + (((p_y + y_pos) % 4) * 2 + (p_core ^ core)) * 8
        + p_row
    )
    (pick,) = tie((source[:, None] == at[None, :]).astype(BF))

    def turn(rows):
        return lax.dot_general(
            pick, rows, (((1,), (1,)), ((), ())), preferred_element_type=F32
        ).astype(BF)

    def products(turned, raw):
        here = turned.reshape(2, 512, -1)[:, :64].reshape(128, -1)
        cross = jnp.dot(here, raw, preferred_element_type=F32)
        return cross, jnp.sum(here.astype(F32), 1)

    def early(rows):
        return jnp.dot(rows, w_early, preferred_element_type=F32).astype(BF)

    half = pixels // 2
    deep = swap(own, "chan")
    right = shift(own, "chan", 1)
    left = shift(own, "chan", 3)
    raw_own = jnp.dot(own, w_early, preferred_element_type=F32)
    sums_e = jnp.stack([jnp.sum(raw_own, 0), jnp.sum(raw_own * raw_own, 0)])
    sums_e = sum_batch(sums_e)
    sums_e, deep, right, left = tie(sums_e, deep, right, left)
    far_0 = shift(right[:half], "chan", 1)
    far_1 = shift(left[half:], "chan", 3)
    sums_e = sum_pair(sums_e, "chan")
    sums_e, far_0, far_1, deep = tie(sums_e, far_0, far_1, deep)
    sums_e = sum_ring(sums_e, "chan")
    deep_right = shift(deep, "chan", 1)
    deep_left = shift(deep, "chan", 3)
    deep_far = swap(jnp.concatenate([far_0, far_1], 0), "chan")
    sums_e, deep_0 = tie(sums_e, deep)
    raw_0 = early(jnp.concatenate([own, right, left, deep_0], 0))
    sums_e, raw_0, far_0, far_1, deep_right, deep_left, deep_far = tie(
        sums_e, raw_0, far_0, far_1, deep_right, deep_left, deep_far
    )
    mean_e = sums_e[0] / count
    rstd_e = lax.rsqrt(sums_e[1] / count - mean_e * mean_e + 1e-05)
    scale_e = rstd_e * gain_early
    offset_e = bias_early - mean_e * scale_e

    order = jnp.stack(
        [
            ((x_pos + dx) % 4) * 2 + (z_pos ^ dz)
            for dx, dz in ((0, 0), (1, 0), (3, 0), (0, 1), (2, 0), (1, 1), (3, 1), (2, 1))
        ]
    ).astype(jnp.int32)

    rest = jnp.concatenate([far_0, far_1, deep_right, deep_left, deep_far], 0)
    raws = [raw_0, early(rest)]
    act_t, slope, late, sums_l = fwd_pass(
        raws, scale_e[None], offset_e[None], w_late
    )
    level = sums_l[2]
    sums_l = sum_pair(sums_l[:2], "batch")
    sums_l, rest, deep = tie(sums_l, rest, deep)
    turned = [turn(jnp.concatenate([own, right, left, deep], 0))]
    sums_l = sum_ring(sums_l, "batch") / count
    sums_l, turned[0], rest = tie(sums_l, turned[0], rest)
    mean_l = sums_l[0]
    rstd_l = lax.rsqrt(sums_l[1] - mean_l * mean_l + 1e-05)
    near_l = mean_l - level
    scale_l = rstd_l * gain_late
    offset_l = bias_late - near_l * scale_l
    late_out, grad_y, back = late_pass(
        order, late, cotangent.reshape(8, pixels, width_out), scale_l, offset_l
    )
    late_out = late_out.reshape(cotangent.shape)

    back = jnp.stack([back[0], back[1] + level * back[0]])
    back = sum_pair(back, "batch")
    back, rest = tie(back, rest)
    turned.append(turn(rest))
    back = sum_ring(back, "batch") / count
    back, *turned = tie(back, *turned)
    back_one = back[0]
    back_two = rstd_l * (back[1] - mean_l * back_one)
    by_late = -scale_l * rstd_l * back_two
    constant = -scale_l * back_one - near_l * by_late

    grad_h = (grad_y.astype(F32) * scale_l + late.astype(F32) * by_late + constant).astype(BF)
    (grad_h,) = tie(grad_h)

    late = weight_grad(act_t, grad_h)
    grad_h, late = tie(grad_h, late)
    late = lax.psum_scatter(late, "batch", tiled=True)
    step = width_mid // 2

    def early_cut(k, grad_h):
        return early_grad(grad_h, turned, w_late, slope, raws, k * step, step)

    term_a = early_cut(0, grad_h)
    grad_h, term_a = tie(grad_h, term_a)
    part_a, sums_a = scatter_pair_sums(term_a, "batch")
    term_b = early_cut(1, grad_h)
    term_b, part_a, sums_a = tie(term_b, part_a, sums_a)
    part_b, sums_b = scatter_pair_sums(term_b, "batch")
    late = sum_pair(late, "section")
    grad = jnp.concatenate([part_a, part_b], 1)
    sums_g = jnp.concatenate([sums_a, sums_b], 1)
    cross, colsum = products(turned[0], raws[0])
    more, columns = products(turned[1], raws[1])
    one, two, three, late, cross, colsum = tie(
        *ring_messages(grad, sums_g), late, cross + more, colsum + columns
    )
    one, two, three = (
        shift(part, "chan", -k) for k, part in ((1, one), (2, two), (3, three))
    )
    late = lax.all_gather(late, "batch", tiled=True)
    cross = jnp.concatenate([cross, jnp.broadcast_to(colsum[:, None], (128, 128))], 1)
    cross = scatter_pair(cross, "batch")
    grad, sums_g = ring_total(grad, sums_g, one, two, three)
    grad, sums_g, cross = tie(grad, sums_g, cross)
    cross = scatter_ring(cross, "batch")
    grad = jnp.concatenate([grad.astype(BF), pack_sums(sums_g)], 0)
    grad, sums_g = scatter_pair_sums(grad, "chan")
    grad = grad.astype(F32)
    grad_late = widen_rows(late)
    colsum = cross[:, width_mid:][:, :1]
    cross = rstd_e * (cross[:, :width_mid] - colsum * mean_e)
    parts = [
        jnp.concatenate([grad[k * 16 : (k + 1) * 16], sums_g], 0) for k in range(4)
    ]
    one, two, three = (shift(parts[k], "batch", -k) for k in (1, 2, 3))
    one, two, three, grad_late = tie(one, two, three, grad_late)
    total = (parts[0] + two) + (one + three)
    grad, sums_g = total[:16], total[16:] / count
    back_one = sums_g[:1]
    back_two = rstd_e * (sums_g[1:] - mean_e * back_one)
    grad = scale_e * (grad - colsum * back_one - cross * back_two)
    grad_early = scatter_pair(grad, "section")
    return (late_out, grad_late, grad_early)


def solution(mesh):
    return jax.shard_map(
        body,
        mesh=mesh,
        in_specs=(
            P("section", "batch", "chan", None, None),
            P(),
            P(),
            P(),
            P(None, "chan"),
            P("chan"),
            P("chan"),
            P("section", "batch", None, "chan"),
        ),
        out_specs=(
            P("section", "batch", None, "chan"),
            P(None, "chan"),
            P(("section", "chan", "batch"), None),
        ),
        check_vma=False,
    )
```

```python
import functools

import jax
import jax.numpy as jnp
from jax import lax
from jax.experimental import pallas as pl
from jax.experimental.pallas import tpu as pltpu
from jax.sharding import PartitionSpec as P

BF = jnp.bfloat16
F32 = jnp.float32
MIB = 1 << 20


def shift(value, axis, step):
    return lax.ppermute(
        value, axis, [(i, ((i // 2 - step) % 4) * 2 + i % 2) for i in range(8)]
    )


def swap(value, axis):
    size = 2 if axis == "section" else 8
    return lax.ppermute(value, axis, [(i, i ^ 1) for i in range(size)])


def sum_pair(value, axis):
    return value + swap(value, axis)


def sum_ring(value, axis):
    one, two, three = (shift(value, axis, step) for step in (1, 2, 3))
    return (value + two) + (one + three)


def sum_batch(value):
    return sum_ring(sum_pair(value, "batch"), "batch")


def scatter_pair(value, axis):
    rows = value.shape[0] // 2
    return value[:rows].astype(F32) + swap(value[rows:], axis).astype(F32)


def scatter_ring(value, axis):
    rows = value.shape[0] // 4
    one, two, three = (
        shift(value[k * rows : (k + 1) * rows], axis, -k).astype(F32) for k in (1, 2, 3)
    )
    return (value[:rows].astype(F32) + two) + (one + three)


def tie(*values):
    return lax.optimization_barrier(values)


def sigmoid(value):
    return 0.5 * jnp.tanh(0.5 * value) + 0.5


def params(mib):
    return pltpu.CompilerParams(vmem_limit_bytes=mib * MIB)


def fwd_kernel(
    raw_0, raw_1, scale, offset, w_late, act_t, slope, late, sums, acts
):
    image = pl.program_id(0)
    for c in range(0, w_late.shape[0], 256):
        at = slice(c, c + 256)
        value = jnp.where(image < 4, raw_0[:, at], raw_1[:, at]).astype(F32)
        pre = (value * scale[:, at] + offset[:, at]).astype(BF)
        sig = sigmoid(pre)
        act = pre * sig
        slope[:, at] = sig + act * (1.0 - sig)
        acts[:, at] = act
        act_t[at, :] = act.T
    for n in range(0, w_late.shape[1], 256):
        at = slice(n, n + 256)
        value = jnp.dot(acts[...], w_late[:, at], preferred_element_type=F32)
        one = jnp.sum(value, 0, keepdims=True)
        two = jnp.sum(value * value, 0, keepdims=True)
        level = jnp.where(image == 0, one / value.shape[0], sums[2:3, at])
        late[:, at] = (value - level).astype(BF)
        sums[0:1, at] = jnp.where(image == 0, 0.0, sums[0:1, at]) + one
        sums[1:2, at] = jnp.where(image == 0, 0.0, sums[1:2, at]) + two
        sums[2:3, at] = level


def fwd_pass(raws, scale, offset, w_late):
    mid, out = w_late.shape
    rows = 2 * raws[0].shape[0]

    return pl.pallas_call(
        fwd_kernel,
        out_shape=(
            jax.ShapeDtypeStruct((mid, rows), BF),
            jax.ShapeDtypeStruct((rows, mid), BF),
            jax.ShapeDtypeStruct((rows, out), BF),
            jax.ShapeDtypeStruct((8, out), F32),
        ),
        grid_spec=pl.GridSpec(
            grid=(8,),
            in_specs=[
                pl.BlockSpec((256, mid), lambda i: (jnp.minimum(i, 3), 0)),
                pl.BlockSpec((256, mid), lambda i: (jnp.maximum(i - 4, 0), 0)),
                pl.BlockSpec((1, mid), lambda i: (0, 0)),
                pl.BlockSpec((1, mid), lambda i: (0, 0)),
                pl.BlockSpec(memory_space=pltpu.VMEM),
            ],
            out_specs=[
                pl.BlockSpec((mid, 256), lambda i: (0, i)),
                pl.BlockSpec((256, mid), lambda i: (i, 0)),
                pl.BlockSpec((256, out), lambda i: (i, 0)),
                pl.BlockSpec((8, out), lambda i: (0, 0)),
            ],
            scratch_shapes=[pltpu.VMEM((256, mid), BF)],
        ),
        cost_estimate=pl.CostEstimate(
            flops=2 * rows * mid * out,
            bytes_accessed=rows * (mid * 6 + out * 2) + 2 * mid * out,
            transcendentals=rows * mid,
        ),
        compiler_params=params(52),
    )(*raws, scale, offset, w_late)


def late_kernel(order, late, cot, scale, offset, out, grad, sums):
    @pl.when(pl.program_id(0) == 0)
    def _():
        sums[...] = jnp.zeros_like(sums)

    def step(k, carry):
        one, two = carry
        at = pl.ds(pl.multiple_of(k * 16, 16), 16)
        value = late[at, :].astype(F32)
        pre = value * scale[...] + offset[...]
        sig = sigmoid(pre)
        gate = pre * sig
        out[0, at, :] = gate.astype(BF)
        grad_y = cot[0, at, :].astype(F32) * (sig + gate * (1.0 - sig))
        grad[at, :] = grad_y.astype(BF)
        both = grad_y * value
        return one + grad_y[:8] + grad_y[8:], two + both[:8] + both[8:]

    zero = jnp.zeros((8, late.shape[1]), F32)
    one, two = lax.fori_loop(0, late.shape[0] // 16, step, (zero, zero), unroll=2)
    sums[0:1] += jnp.sum(one, 0, keepdims=True)
    sums[1:2] += jnp.sum(two, 0, keepdims=True)


def late_pass(order, late, cot, scale, offset):
    rows, width = late.shape
    vector = pl.BlockSpec((1, width), lambda i, o: (0, 0))
    return pl.pallas_call(
        late_kernel,
        out_shape=(
            jax.ShapeDtypeStruct(cot.shape, BF),
            jax.ShapeDtypeStruct((rows, width), BF),
            jax.ShapeDtypeStruct((8, width), F32),
        ),
        grid_spec=pltpu.PrefetchScalarGridSpec(
            num_scalar_prefetch=1,
            grid=(rows // 256,),
            in_specs=[
                pl.BlockSpec((256, width), lambda i, o: (i, 0)),
                pl.BlockSpec((1, 256, width), lambda i, o: (o[i], 0, 0)),
                vector,
                vector,
            ],
            out_specs=[
                pl.BlockSpec((1, 256, width), lambda i, o: (o[i], 0, 0)),
                pl.BlockSpec((256, width), lambda i, o: (i, 0)),
                pl.BlockSpec((8, width), lambda i, o: (0, 0)),
            ],
        ),
        cost_estimate=pl.CostEstimate(
            flops=16 * rows * width, bytes_accessed=rows * width * 8, transcendentals=rows * width
        ),
        compiler_params=params(24),
    )(order, late, cot, scale[None], offset[None])


def weight_kernel(turned, grad_h, out):
    for n in range(0, out.shape[1], 256):
        out[:, n : n + 256] = jnp.dot(
            turned[...], grad_h[:, n : n + 256], preferred_element_type=F32
        ).astype(BF)


def weight_grad(turned, grad_h):
    depth, rows = turned.shape
    width = grad_h.shape[1]
    return pl.pallas_call(
        weight_kernel,
        grid=(depth // 512,),
        out_shape=jax.ShapeDtypeStruct((depth, width), BF),
        in_specs=[
            pl.BlockSpec((512, rows), lambda i: (i, 0)),
            pl.BlockSpec(memory_space=pltpu.VMEM),
        ],
        out_specs=pl.BlockSpec((512, width), lambda i: (i, 0)),
        cost_estimate=pl.CostEstimate(
            flops=2 * depth * rows * width,
            bytes_accessed=2 * (depth * rows + rows * width + depth * width),
            transcendentals=0,
        ),
        compiler_params=params(40),
    )(turned, grad_h)


def early_kernel(
    grad_h, turned_0, turned_1, raw_0, raw_1, slope, w_late, term, grad_pre
):
    depth, cut = turned_0.shape
    one = two = 0.0
    for r in range(0, grad_h.shape[0], 512):
        at = slice(r, r + 512)
        grad = lax.dot_general(
            grad_h[at, :], w_late[...], (((1,), (1,)), ((), ())), preferred_element_type=F32
        )
        grad = grad * slope[at, :].astype(F32)
        one += jnp.sum(grad, 0, keepdims=True)
        raw = (raw_0 if r < cut else raw_1)[r % cut : r % cut + 512, :]
        two += jnp.sum(grad * raw.astype(F32), 0, keepdims=True)
        grad_pre[at, :] = grad.astype(BF)
    one_high, two_high = one.astype(BF), two.astype(BF)
    term[depth : depth + 16, :] = jnp.concatenate(
        [
            one_high,
            two_high,
            (one - one_high.astype(F32)).astype(BF),
            (two - two_high.astype(F32)).astype(BF),
            jnp.zeros((12, term.shape[1]), BF),
        ],
        0,
    )
    for m in range(0, depth, 512):
        term[m : m + 512, :] = (
            jnp.dot(turned_0[m : m + 512, :], grad_pre[:cut, :], preferred_element_type=F32)
            + jnp.dot(turned_1[m : m + 512, :], grad_pre[cut:, :], preferred_element_type=F32)
        ).astype(BF)


def early_grad(grad_h, turned, w_late, slope, raws, first, width):
    rows, out = grad_h.shape
    depth = turned[0].shape[0]
    tile = 256
    base = first // tile
    column = pl.BlockSpec((rows, tile), lambda j: (0, j + base))
    half = pl.BlockSpec((rows // 2, tile), lambda j: (0, j + base))
    return pl.pallas_call(
        early_kernel,
        grid=(width // tile,),
        out_shape=jax.ShapeDtypeStruct((depth + 16, width), BF),
        in_specs=[pl.BlockSpec(memory_space=pltpu.VMEM)] * 3
        + [half, half, column, pl.BlockSpec((tile, out), lambda j: (j + base, 0))],
        out_specs=pl.BlockSpec((depth + 16, tile), lambda j: (0, j)),
        scratch_shapes=[pltpu.VMEM((rows, tile), BF)],
        cost_estimate=pl.CostEstimate(
            flops=2 * rows * width * (out + depth),
            bytes_accessed=2 * (rows * out + rows * depth + 4 * rows * width),
            transcendentals=0,
        ),
        compiler_params=params(40),
    )(grad_h, *turned, *raws, slope, w_late)


def widen_kernel(value, out):
    out[...] = value[...].astype(F32)


def widen_rows(value):
    rows, width = value.shape
    return pl.pallas_call(
        widen_kernel,
        grid=(8,),
        out_shape=jax.ShapeDtypeStruct((rows, width), F32),
        in_specs=[pl.BlockSpec((256, width), lambda i: (i, 0))],
        out_specs=pl.BlockSpec((256, width), lambda i: (i, 0)),
        cost_estimate=pl.CostEstimate(flops=0, bytes_accessed=rows * width * 6, transcendentals=0),
        compiler_params=params(56),
    )(value)


def pack_sums(sums):
    high = lax.reduce_precision(sums, 8, 7)
    rows = jnp.concatenate([high, sums - high], 0).astype(BF)
    return jnp.pad(rows, ((0, 12), (0, 0)))


def unpack_sums(rows):
    return rows[0:2].astype(F32) + rows[2:4].astype(F32)


def scatter_pair_sums(value, axis):
    half = (value.shape[0] - 16) // 2
    other = swap(value[half:], axis)
    total = value[:half].astype(F32) + other[:half].astype(F32)
    return total.astype(BF), unpack_sums(value[2 * half :]) + unpack_sums(other[half:])


def ring_messages(value, sums):
    rows = value.shape[0] // 4
    packed = pack_sums(sums)
    return [
        jnp.concatenate([value[k * rows : (k + 1) * rows], packed], 0) for k in (1, 2, 3)
    ]


def ring_total(value, sums, one, two, three):
    rows = value.shape[0] // 4
    total = (value[:rows].astype(F32) + two[:rows].astype(F32)) + (
        one[:rows].astype(F32) + three[:rows].astype(F32)
    )
    return total, (sums + unpack_sums(two[rows:])) + (
        unpack_sums(one[rows:]) + unpack_sums(three[rows:])
    )


def body(images, w_early, gain_early, bias_early, w_late, gain_late, bias_late, cotangent):
    width_in, width_mid = w_early.shape
    width_out = w_late.shape[1]
    pixels = images.shape[3]
    own = images.reshape(pixels, width_in)
    chan = lax.axis_index("chan")
    batch = lax.axis_index("batch")
    section = lax.axis_index("section")
    x_pos, z_pos = chan // 2, chan % 2
    y_pos, core = batch // 2, batch % 2
    count = float(pixels * 64)

    at = jnp.arange(width_in, dtype=jnp.int32)
    p_core, p_x, p_z = at // 512, (at // 128) % 4, (at // 64) % 2
    p_y, p_sec, p_row = (at // 16) % 4, (at // 8) % 2, at % 8
    source = (
        (p_sec ^ section) * 512
        + (((p_x + x_pos) % 4) * 2 + (p_z ^ z_pos)) * 64
        + (((p_y + y_pos) % 4) * 2 + (p_core ^ core)) * 8
        + p_row
    )
    (pick,) = tie((source[:, None] == at[None, :]).astype(BF))

    def turn(rows):
        return lax.dot_general(
            pick, rows, (((1,), (1,)), ((), ())), preferred_element_type=F32
        ).astype(BF)

    def products(turned, raw):
        here = turned.reshape(2, 512, -1)[:, :64].reshape(128, -1)
        cross = jnp.dot(here, raw, preferred_element_type=F32)
        return cross, jnp.sum(here.astype(F32), 1)

    def early(rows):
        return jnp.dot(rows, w_early, preferred_element_type=F32).astype(BF)

    half = pixels // 2
    deep = swap(own, "chan")
    right = shift(own, "chan", 1)
    left = shift(own, "chan", 3)
    raw_own = jnp.dot(own, w_early, preferred_element_type=F32)
    sums_e = jnp.stack([jnp.sum(raw_own, 0), jnp.sum(raw_own * raw_own, 0)])
    sums_e = sum_batch(sums_e)
    sums_e, deep, right, left = tie(sums_e, deep, right, left)
    far_0 = shift(right[:half], "chan", 1)
    far_1 = shift(left[half:], "chan", 3)
    sums_e = sum_pair(sums_e, "chan")
    sums_e, far_0, far_1, deep = tie(sums_e, far_0, far_1, deep)
    sums_e = sum_ring(sums_e, "chan")
    deep_right = shift(deep, "chan", 1)
    deep_left = shift(deep, "chan", 3)
    deep_far = swap(jnp.concatenate([far_0, far_1], 0), "chan")
    sums_e, deep_0 = tie(sums_e, deep)
    raw_0 = early(jnp.concatenate([own, right, left, deep_0], 0))
    sums_e, raw_0, far_0, far_1, deep_right, deep_left, deep_far = tie(
        sums_e, raw_0, far_0, far_1, deep_right, deep_left, deep_far
    )
    mean_e = sums_e[0] / count
    rstd_e = lax.rsqrt(sums_e[1] / count - mean_e * mean_e + 1e-05)
    scale_e = rstd_e * gain_early
    offset_e = bias_early - mean_e * scale_e

    order = jnp.stack(
        [
            ((x_pos + dx) % 4) * 2 + (z_pos ^ dz)
            for dx, dz in ((0, 0), (1, 0), (3, 0), (0, 1), (2, 0), (1, 1), (3, 1), (2, 1))
        ]
    ).astype(jnp.int32)

    rest = jnp.concatenate([far_0, far_1, deep_right, deep_left, deep_far], 0)
    raws = [raw_0, early(rest)]
    act_t, slope, late, sums_l = fwd_pass(
        raws, scale_e[None], offset_e[None], w_late
    )
    level = sums_l[2]
    sums_l = sum_pair(sums_l[:2], "batch")
    sums_l, rest, deep = tie(sums_l, rest, deep)
    turned = [turn(jnp.concatenate([own, right, left, deep], 0))]
    sums_l = sum_ring(sums_l, "batch") / count
    sums_l, turned[0], rest = tie(sums_l, turned[0], rest)
    mean_l = sums_l[0]
    rstd_l = lax.rsqrt(sums_l[1] - mean_l * mean_l + 1e-05)
    near_l = mean_l - level
    scale_l = rstd_l * gain_late
    offset_l = bias_late - near_l * scale_l
    late_out, grad_y, back = late_pass(
        order, late, cotangent.reshape(8, pixels, width_out), scale_l, offset_l
    )
    late_out = late_out.reshape(cotangent.shape)

    back = jnp.stack([back[0], back[1] + level * back[0]])
    back = sum_pair(back, "batch")
    back, rest = tie(back, rest)
    turned.append(turn(rest))
    back = sum_ring(back, "batch") / count
    back, *turned = tie(back, *turned)
    back_one = back[0]
    back_two = rstd_l * (back[1] - mean_l * back_one)
    by_late = -scale_l * rstd_l * back_two
    constant = -scale_l * back_one - near_l * by_late

    grad_h = (grad_y.astype(F32) * scale_l + late.astype(F32) * by_late + constant).astype(BF)
    (grad_h,) = tie(grad_h)

    late = weight_grad(act_t, grad_h)
    grad_h, late = tie(grad_h, late)
    late = lax.psum_scatter(late, "batch", tiled=True)
    step = width_mid // 4

    def early_cut(first, count, grad_h):
        return early_grad(grad_h, turned, w_late, slope, raws, first * step, count * step)

    def to_owners(messages):
        return [shift(part, "chan", -k) for k, part in zip((1, 2, 3), messages)]

    term_a = early_cut(0, 2, grad_h)
    grad_h, term_a = tie(grad_h, term_a)
    part_a, sums_a = scatter_pair_sums(term_a, "batch")
    term_b = early_cut(2, 1, grad_h)
    grad_h, term_b, part_a, sums_a, *sent = tie(
        grad_h, term_b, part_a, sums_a, *ring_messages(part_a, sums_a)
    )
    sent = to_owners(sent)
    term_c = early_cut(3, 1, grad_h)
    term_b, term_c, *sent = tie(term_b, term_c, *sent)
    part_a, sums_a = ring_total(part_a, sums_a, *sent)
    part_b, sums_b = scatter_pair_sums(jnp.concatenate([term_b, term_c], 1), "batch")
    late = sum_pair(late, "section")
    late, *sent = tie(late, *ring_messages(part_b, sums_b))
    late = lax.all_gather(late, "batch", tiled=True)
    one, two, three = to_owners(sent)
    two, *turned = tie(two, *turned)
    cross, colsum = products(turned[0], raws[0])
    more, columns = products(turned[1], raws[1])
    cross, colsum = cross + more, colsum + columns
    cross = jnp.concatenate([cross, jnp.broadcast_to(colsum[:, None], (128, 128))], 1)
    cross = scatter_pair(cross, "batch")
    part_b, sums_b = ring_total(part_b, sums_b, one, two, three)
    grad = jnp.concatenate([part_a, part_b], 1)
    sums_g = jnp.concatenate([sums_a, sums_b], 1)
    grad, sums_g, cross = tie(grad, sums_g, cross)
    cross = scatter_ring(cross, "batch")
    grad = jnp.concatenate([grad.astype(BF), pack_sums(sums_g)], 0)
    grad, sums_g = scatter_pair_sums(grad, "chan")
    grad = grad.astype(F32)
    grad_late = widen_rows(late)
    colsum = cross[:, width_mid:][:, :1]
    cross = rstd_e * (cross[:, :width_mid] - colsum * mean_e)
    parts = [
        jnp.concatenate([grad[k * 16 : (k + 1) * 16], sums_g], 0) for k in range(4)
    ]
    one, two, three = (shift(parts[k], "batch", -k) for k in (1, 2, 3))
    one, two, three, grad_late = tie(one, two, three, grad_late)
    total = (parts[0] + two) + (one + three)
    grad, sums_g = total[:16], total[16:] / count
    back_one = sums_g[:1]
    back_two = rstd_e * (sums_g[1:] - mean_e * back_one)
    grad = scale_e * (grad - colsum * back_one - cross * back_two)
    grad_early = scatter_pair(grad, "section")
    return (late_out, grad_late, grad_early)


def solution(mesh):
    return jax.shard_map(
        body,
        mesh=mesh,
        in_specs=(
            P("section", "batch", "chan", None, None),
            P(),
            P(),
            P(),
            P(None, "chan"),
            P("chan"),
            P("chan"),
            P("section", "batch", None, "chan"),
        ),
        out_specs=(
            P("section", "batch", None, "chan"),
            P(None, "chan"),
            P(("section", "chan", "batch"), None),
        ),
        check_vma=False,
    )
```

```python
import functools

import jax
import jax.numpy as jnp
from jax import lax
from jax.experimental import pallas as pl
from jax.experimental.pallas import tpu as pltpu
from jax.sharding import PartitionSpec as P

BF = jnp.bfloat16
F32 = jnp.float32
MIB = 1 << 20


def shift(value, axis, step):
    return lax.ppermute(
        value, axis, [(i, ((i // 2 - step) % 4) * 2 + i % 2) for i in range(8)]
    )


def swap(value, axis):
    size = 2 if axis == "section" else 8
    return lax.ppermute(value, axis, [(i, i ^ 1) for i in range(size)])


def sum_pair(value, axis):
    return value + swap(value, axis)


def sum_ring(value, axis):
    one, two, three = (shift(value, axis, step) for step in (1, 2, 3))
    return (value + two) + (one + three)


def sum_batch(value):
    return sum_ring(sum_pair(value, "batch"), "batch")


def scatter_pair(value, axis):
    rows = value.shape[0] // 2
    return value[:rows].astype(F32) + swap(value[rows:], axis).astype(F32)


def scatter_ring(value, axis):
    rows = value.shape[0] // 4
    one, two, three = (
        shift(value[k * rows : (k + 1) * rows], axis, -k).astype(F32) for k in (1, 2, 3)
    )
    return (value[:rows].astype(F32) + two) + (one + three)


def tie(*values):
    return lax.optimization_barrier(values)


def sigmoid(value):
    return 0.5 * jnp.tanh(0.5 * value) + 0.5


def params(mib):
    return pltpu.CompilerParams(vmem_limit_bytes=mib * MIB)


def fwd_kernel(
    raw_0, raw_1, scale, offset, w_late, act_t, slope, late, sums, acts
):
    image = pl.program_id(0)
    for c in range(0, w_late.shape[0], 256):
        at = slice(c, c + 256)
        value = jnp.where(image < 4, raw_0[:, at], raw_1[:, at]).astype(F32)
        pre = (value * scale[:, at] + offset[:, at]).astype(BF)
        sig = sigmoid(pre)
        act = pre * sig
        slope[:, at] = sig + act * (1.0 - sig)
        acts[:, at] = act
        act_t[at, :] = act.T
    for n in range(0, w_late.shape[1], 256):
        at = slice(n, n + 256)
        value = jnp.dot(acts[...], w_late[:, at], preferred_element_type=F32)
        one = jnp.sum(value, 0, keepdims=True)
        two = jnp.sum(value * value, 0, keepdims=True)
        level = jnp.where(image == 0, one / value.shape[0], sums[2:3, at])
        late[:, at] = (value - level).astype(BF)
        sums[0:1, at] = jnp.where(image == 0, 0.0, sums[0:1, at]) + one
        sums[1:2, at] = jnp.where(image == 0, 0.0, sums[1:2, at]) + two
        sums[2:3, at] = level


def fwd_pass(raws, scale, offset, w_late):
    mid, out = w_late.shape
    rows = 2 * raws[0].shape[0]

    return pl.pallas_call(
        fwd_kernel,
        out_shape=(
            jax.ShapeDtypeStruct((mid, rows), BF),
            jax.ShapeDtypeStruct((rows, mid), BF),
            jax.ShapeDtypeStruct((rows, out), BF),
            jax.ShapeDtypeStruct((8, out), F32),
        ),
        grid_spec=pl.GridSpec(
            grid=(8,),
            in_specs=[
                pl.BlockSpec((256, mid), lambda i: (jnp.minimum(i, 3), 0)),
                pl.BlockSpec((256, mid), lambda i: (jnp.maximum(i - 4, 0), 0)),
                pl.BlockSpec((1, mid), lambda i: (0, 0)),
                pl.BlockSpec((1, mid), lambda i: (0, 0)),
                pl.BlockSpec(memory_space=pltpu.VMEM),
            ],
            out_specs=[
                pl.BlockSpec((mid, 256), lambda i: (0, i)),
                pl.BlockSpec((256, mid), lambda i: (i, 0)),
                pl.BlockSpec((256, out), lambda i: (i, 0)),
                pl.BlockSpec((8, out), lambda i: (0, 0)),
            ],
            scratch_shapes=[pltpu.VMEM((256, mid), BF)],
        ),
        cost_estimate=pl.CostEstimate(
            flops=2 * rows * mid * out,
            bytes_accessed=rows * (mid * 6 + out * 2) + 2 * mid * out,
            transcendentals=rows * mid,
        ),
        compiler_params=params(52),
    )(*raws, scale, offset, w_late)


def late_kernel(order, late, cot, scale, offset, out, grad, sums):
    @pl.when(pl.program_id(0) == 0)
    def _():
        sums[...] = jnp.zeros_like(sums)

    def step(k, carry):
        one, two = carry
        at = pl.ds(pl.multiple_of(k * 16, 16), 16)
        value = late[at, :].astype(F32)
        pre = value * scale[...] + offset[...]
        sig = sigmoid(pre)
        gate = pre * sig
        out[0, at, :] = gate.astype(BF)
        grad_y = cot[0, at, :].astype(F32) * (sig + gate * (1.0 - sig))
        grad[at, :] = grad_y.astype(BF)
        both = grad_y * value
        return one + grad_y[:8] + grad_y[8:], two + both[:8] + both[8:]

    zero = jnp.zeros((8, late.shape[1]), F32)
    one, two = lax.fori_loop(0, late.shape[0] // 16, step, (zero, zero), unroll=2)
    sums[0:1] += jnp.sum(one, 0, keepdims=True)
    sums[1:2] += jnp.sum(two, 0, keepdims=True)


def late_pass(order, late, cot, scale, offset):
    rows, width = late.shape
    vector = pl.BlockSpec((1, width), lambda i, o: (0, 0))
    return pl.pallas_call(
        late_kernel,
        out_shape=(
            jax.ShapeDtypeStruct(cot.shape, BF),
            jax.ShapeDtypeStruct((rows, width), BF),
            jax.ShapeDtypeStruct((8, width), F32),
        ),
        grid_spec=pltpu.PrefetchScalarGridSpec(
            num_scalar_prefetch=1,
            grid=(rows // 256,),
            in_specs=[
                pl.BlockSpec((256, width), lambda i, o: (i, 0)),
                pl.BlockSpec((1, 256, width), lambda i, o: (o[i], 0, 0)),
                vector,
                vector,
            ],
            out_specs=[
                pl.BlockSpec((1, 256, width), lambda i, o: (o[i], 0, 0)),
                pl.BlockSpec((256, width), lambda i, o: (i, 0)),
                pl.BlockSpec((8, width), lambda i, o: (0, 0)),
            ],
        ),
        cost_estimate=pl.CostEstimate(
            flops=16 * rows * width, bytes_accessed=rows * width * 8, transcendentals=rows * width
        ),
        compiler_params=params(24),
    )(order, late, cot, scale[None], offset[None])


def weight_kernel(turned, grad_h, out):
    for n in range(0, out.shape[1], 256):
        out[:, n : n + 256] = jnp.dot(
            turned[...], grad_h[:, n : n + 256], preferred_element_type=F32
        ).astype(BF)


def weight_grad(turned, grad_h):
    depth, rows = turned.shape
    width = grad_h.shape[1]
    return pl.pallas_call(
        weight_kernel,
        grid=(depth // 512,),
        out_shape=jax.ShapeDtypeStruct((depth, width), BF),
        in_specs=[
            pl.BlockSpec((512, rows), lambda i: (i, 0)),
            pl.BlockSpec(memory_space=pltpu.VMEM),
        ],
        out_specs=pl.BlockSpec((512, width), lambda i: (i, 0)),
        cost_estimate=pl.CostEstimate(
            flops=2 * depth * rows * width,
            bytes_accessed=2 * (depth * rows + rows * width + depth * width),
            transcendentals=0,
        ),
        compiler_params=params(40),
    )(turned, grad_h)


def early_kernel(
    grad_h, turned_0, turned_1, raw_0, raw_1, slope, w_late, term, grad_pre
):
    depth, cut = turned_0.shape
    one = two = 0.0
    for r in range(0, grad_h.shape[0], 512):
        at = slice(r, r + 512)
        grad = lax.dot_general(
            grad_h[at, :], w_late[...], (((1,), (1,)), ((), ())), preferred_element_type=F32
        )
        grad = grad * slope[at, :].astype(F32)
        one += jnp.sum(grad, 0, keepdims=True)
        raw = (raw_0 if r < cut else raw_1)[r % cut : r % cut + 512, :]
        two += jnp.sum(grad * raw.astype(F32), 0, keepdims=True)
        grad_pre[at, :] = grad.astype(BF)
    one_high, two_high = one.astype(BF), two.astype(BF)
    term[depth : depth + 16, :] = jnp.concatenate(
        [
            one_high,
            two_high,
            (one - one_high.astype(F32)).astype(BF),
            (two - two_high.astype(F32)).astype(BF),
            jnp.zeros((12, term.shape[1]), BF),
        ],
        0,
    )
    for m in range(0, depth, 1024):
        term[m : m + 1024, :] = (
            jnp.dot(turned_0[m : m + 1024, :], grad_pre[:cut, :], preferred_element_type=F32)
            + jnp.dot(turned_1[m : m + 1024, :], grad_pre[cut:, :], preferred_element_type=F32)
        ).astype(BF)


def early_grad(grad_h, turned, w_late, slope, raws, first, width):
    rows, out = grad_h.shape
    depth = turned[0].shape[0]
    tile = 256
    base = first // tile
    column = pl.BlockSpec((rows, tile), lambda j: (0, j + base))
    half = pl.BlockSpec((rows // 2, tile), lambda j: (0, j + base))
    return pl.pallas_call(
        early_kernel,
        grid=(width // tile,),
        out_shape=jax.ShapeDtypeStruct((depth + 16, width), BF),
        in_specs=[pl.BlockSpec(memory_space=pltpu.VMEM)] * 3
        + [half, half, column, pl.BlockSpec((tile, out), lambda j: (j + base, 0))],
        out_specs=pl.BlockSpec((depth + 16, tile), lambda j: (0, j)),
        scratch_shapes=[pltpu.VMEM((rows, tile), BF)],
        cost_estimate=pl.CostEstimate(
            flops=2 * rows * width * (out + depth),
            bytes_accessed=2 * (rows * out + rows * depth + 4 * rows * width),
            transcendentals=0,
        ),
        compiler_params=params(40),
    )(grad_h, *turned, *raws, slope, w_late)


def widen_kernel(value, out):
    out[...] = value[...].astype(F32)


def widen_rows(value):
    rows, width = value.shape
    return pl.pallas_call(
        widen_kernel,
        grid=(8,),
        out_shape=jax.ShapeDtypeStruct((rows, width), F32),
        in_specs=[pl.BlockSpec((256, width), lambda i: (i, 0))],
        out_specs=pl.BlockSpec((256, width), lambda i: (i, 0)),
        cost_estimate=pl.CostEstimate(flops=0, bytes_accessed=rows * width * 6, transcendentals=0),
        compiler_params=params(56),
    )(value)


def pack_sums(sums):
    high = lax.reduce_precision(sums, 8, 7)
    rows = jnp.concatenate([high, sums - high], 0).astype(BF)
    return jnp.pad(rows, ((0, 12), (0, 0)))


def unpack_sums(rows):
    return rows[0:2].astype(F32) + rows[2:4].astype(F32)


def scatter_pair_sums(value, axis):
    half = (value.shape[0] - 16) // 2
    other = swap(value[half:], axis)
    total = value[:half].astype(F32) + other[:half].astype(F32)
    return total.astype(BF), unpack_sums(value[2 * half :]) + unpack_sums(other[half:])


def ring_messages(value, sums):
    rows = value.shape[0] // 4
    packed = pack_sums(sums)
    return [
        jnp.concatenate([value[k * rows : (k + 1) * rows], packed], 0) for k in (1, 2, 3)
    ]


def ring_total(value, sums, one, two, three):
    rows = value.shape[0] // 4
    total = (value[:rows].astype(F32) + two[:rows].astype(F32)) + (
        one[:rows].astype(F32) + three[:rows].astype(F32)
    )
    return total, (sums + unpack_sums(two[rows:])) + (
        unpack_sums(one[rows:]) + unpack_sums(three[rows:])
    )


def body(images, w_early, gain_early, bias_early, w_late, gain_late, bias_late, cotangent):
    width_in, width_mid = w_early.shape
    width_out = w_late.shape[1]
    pixels = images.shape[3]
    own = images.reshape(pixels, width_in)
    chan = lax.axis_index("chan")
    batch = lax.axis_index("batch")
    section = lax.axis_index("section")
    x_pos, z_pos = chan // 2, chan % 2
    y_pos, core = batch // 2, batch % 2
    count = float(pixels * 64)

    at = jnp.arange(width_in, dtype=jnp.int32)
    p_core, p_x, p_z = at // 512, (at // 128) % 4, (at // 64) % 2
    p_y, p_sec, p_row = (at // 16) % 4, (at // 8) % 2, at % 8
    source = (
        (p_sec ^ section) * 512
        + (((p_x + x_pos) % 4) * 2 + (p_z ^ z_pos)) * 64
        + (((p_y + y_pos) % 4) * 2 + (p_core ^ core)) * 8
        + p_row
    )
    (pick,) = tie((source[:, None] == at[None, :]).astype(BF))

    def turn(rows):
        return lax.dot_general(
            pick, rows, (((1,), (1,)), ((), ())), preferred_element_type=F32
        ).astype(BF)

    def products(turned, raw):
        here = turned.reshape(2, 512, -1)[:, :64].reshape(128, -1)
        cross = jnp.dot(here, raw, preferred_element_type=F32)
        return cross, jnp.sum(here.astype(F32), 1)

    def early(rows):
        return jnp.dot(rows, w_early, preferred_element_type=F32).astype(BF)

    half = pixels // 2
    deep = swap(own, "chan")
    right = shift(own, "chan", 1)
    left = shift(own, "chan", 3)
    raw_own = jnp.dot(own, w_early, preferred_element_type=F32)
    sums_e = jnp.stack([jnp.sum(raw_own, 0), jnp.sum(raw_own * raw_own, 0)])
    sums_e = sum_batch(sums_e)
    sums_e, deep, right, left = tie(sums_e, deep, right, left)
    far_0 = shift(right[:half], "chan", 1)
    far_1 = shift(left[half:], "chan", 3)
    sums_e = sum_pair(sums_e, "chan")
    sums_e, far_0, far_1, deep = tie(sums_e, far_0, far_1, deep)
    sums_e = sum_ring(sums_e, "chan")
    deep_right = shift(deep, "chan", 1)
    deep_left = shift(deep, "chan", 3)
    deep_far = swap(jnp.concatenate([far_0, far_1], 0), "chan")
    sums_e, deep_0 = tie(sums_e, deep)
    raw_0 = early(jnp.concatenate([own, right, left, deep_0], 0))
    sums_e, raw_0, far_0, far_1, deep_right, deep_left, deep_far = tie(
        sums_e, raw_0, far_0, far_1, deep_right, deep_left, deep_far
    )
    mean_e = sums_e[0] / count
    rstd_e = lax.rsqrt(sums_e[1] / count - mean_e * mean_e + 1e-05)
    scale_e = rstd_e * gain_early
    offset_e = bias_early - mean_e * scale_e

    order = jnp.stack(
        [
            ((x_pos + dx) % 4) * 2 + (z_pos ^ dz)
            for dx, dz in ((0, 0), (1, 0), (3, 0), (0, 1), (2, 0), (1, 1), (3, 1), (2, 1))
        ]
    ).astype(jnp.int32)

    rest = jnp.concatenate([far_0, far_1, deep_right, deep_left, deep_far], 0)
    raws = [raw_0, early(rest)]
    act_t, slope, late, sums_l = fwd_pass(
        raws, scale_e[None], offset_e[None], w_late
    )
    level = sums_l[2]
    sums_l = sum_pair(sums_l[:2], "batch")
    sums_l, rest, deep = tie(sums_l, rest, deep)
    turned = [turn(jnp.concatenate([own, right, left, deep], 0))]
    sums_l = sum_ring(sums_l, "batch") / count
    sums_l, turned[0], rest = tie(sums_l, turned[0], rest)
    mean_l = sums_l[0]
    rstd_l = lax.rsqrt(sums_l[1] - mean_l * mean_l + 1e-05)
    near_l = mean_l - level
    scale_l = rstd_l * gain_late
    offset_l = bias_late - near_l * scale_l
    late_out, grad_y, back = late_pass(
        order, late, cotangent.reshape(8, pixels, width_out), scale_l, offset_l
    )
    late_out = late_out.reshape(cotangent.shape)

    back = jnp.stack([back[0], back[1] + level * back[0]])
    back = sum_pair(back, "batch")
    back, rest = tie(back, rest)
    turned.append(turn(rest))
    back = sum_ring(back, "batch") / count
    back, *turned = tie(back, *turned)
    back_one = back[0]
    back_two = rstd_l * (back[1] - mean_l * back_one)
    by_late = -scale_l * rstd_l * back_two
    constant = -scale_l * back_one - near_l * by_late

    grad_h = (grad_y.astype(F32) * scale_l + late.astype(F32) * by_late + constant).astype(BF)
    (grad_h,) = tie(grad_h)

    late = weight_grad(act_t, grad_h)
    grad_h, late = tie(grad_h, late)
    late = lax.psum_scatter(late, "batch", tiled=True)
    step = width_mid // 4

    def early_cut(first, count, grad_h):
        return early_grad(grad_h, turned, w_late, slope, raws, first * step, count * step)

    def to_owners(messages):
        return [shift(part, "chan", -k) for k, part in zip((1, 2, 3), messages)]

    term_a = early_cut(0, 2, grad_h)
    grad_h, term_a = tie(grad_h, term_a)
    part_a, sums_a = scatter_pair_sums(term_a, "batch")
    term_b = early_cut(2, 1, grad_h)
    grad_h, term_b, part_a, sums_a, *sent = tie(
        grad_h, term_b, part_a, sums_a, *ring_messages(part_a, sums_a)
    )
    sent = to_owners(sent)
    term_c = early_cut(3, 1, grad_h)
    term_b, term_c, *sent = tie(term_b, term_c, *sent)
    part_a, sums_a = ring_total(part_a, sums_a, *sent)
    part_b, sums_b = scatter_pair_sums(jnp.concatenate([term_b, term_c], 1), "batch")
    late = sum_pair(late, "section")
    late, *sent = tie(late, *ring_messages(part_b, sums_b))
    late = lax.all_gather(late, "batch", tiled=True)
    one, two, three = to_owners(sent)
    two, *turned = tie(two, *turned)
    cross, colsum = products(turned[0], raws[0])
    more, columns = products(turned[1], raws[1])
    cross, colsum = cross + more, colsum + columns
    cross = jnp.concatenate([cross, jnp.broadcast_to(colsum[:, None], (128, 128))], 1)
    cross = scatter_pair(cross, "batch")
    part_b, sums_b = ring_total(part_b, sums_b, one, two, three)
    grad = jnp.concatenate([part_a, part_b], 1)
    sums_g = jnp.concatenate([sums_a, sums_b], 1)
    grad, sums_g, cross = tie(grad, sums_g, cross)
    colsum = cross[:, width_mid:]
    high = lax.reduce_precision(colsum, 8, 7)
    cross = rstd_e * (cross[:, :width_mid] - colsum[:, :1] * mean_e)
    cross = jnp.concatenate([cross, high, colsum - high], 1).astype(BF)
    cross = scatter_ring(cross, "batch")
    grad = jnp.concatenate([grad.astype(BF), pack_sums(sums_g)], 0)
    grad, sums_g = scatter_pair_sums(grad, "chan")
    grad = grad.astype(F32)
    grad_late = widen_rows(late)
    colsum = cross[:, width_mid : width_mid + 1] + cross[:, width_mid + 128 : width_mid + 129]
    cross = cross[:, :width_mid]
    parts = [
        jnp.concatenate([grad[k * 16 : (k + 1) * 16], sums_g], 0) for k in range(4)
    ]
    one, two, three = (shift(parts[k], "batch", -k) for k in (1, 2, 3))
    one, two, three, grad_late = tie(one, two, three, grad_late)
    total = (parts[0] + two) + (one + three)
    grad, sums_g = total[:16], total[16:] / count
    back_one = sums_g[:1]
    back_two = rstd_e * (sums_g[1:] - mean_e * back_one)
    grad = scale_e * (grad - colsum * back_one - cross * back_two)
    grad_early = scatter_pair(grad, "section")
    return (late_out, grad_late, grad_early)


def solution(mesh):
    return jax.shard_map(
        body,
        mesh=mesh,
        in_specs=(
            P("section", "batch", "chan", None, None),
            P(),
            P(),
            P(),
            P(None, "chan"),
            P("chan"),
            P("chan"),
            P("section", "batch", None, "chan"),
        ),
        out_specs=(
            P("section", "batch", None, "chan"),
            P(None, "chan"),
            P(("section", "chan", "batch"), None),
        ),
        check_vma=False,
    )
```
